32 devices in a mesh: det: 8 (over z, x), row: 4 (over y, core).
Axes of the slice: x: 2, y: 2, z: 4, core: 2. Of those that a mesh axis runs over, the one named last changes fastest.
Arguments:
- images: bfloat16 [48, 3, 384, 384], P('det', None, 'row'), may hold values from -6 to 6
- warp_rows: bfloat16 [48, 3, 384, 384], P('det', None, 'row'), may hold values from -0.3125 to 0.3125
- warp_cols: bfloat16 [48, 3, 384, 384], P('det'), may hold values from -0.3125 to 0.3125
- psf_coef: float32 [48, 3, 21], P('det'), may hold values from -1.25 to 1.25
- taps: float32 [21, 21], replicated, may hold values from -1.25 to 1.25
- dest_patch: int32 [432, 1], replicated, may hold values from 0 to 7; in each aligned block of 54 rows (0 to 53, 54 to 107, ...) at most 14 rows name the same one
- dest_block: int32 [432], replicated, may hold values from 0 to 2
- weight_index: int32 [48, 3], replicated, may hold values from 0 to 7
- weight_table: float32 [8], replicated, may hold values from 0.25 to 4
- patch_home: int32 [8], replicated, may hold values from 0 to 7, each once
Outputs:
- difference: bfloat16 [48, 3, 384, 384], P('det', None, 'row')
- coadd: bfloat16 [8, 384, 384], P('det', 'row')
The draws below stay inside these ranges and needn't reach their ends.
Inputs may be any that keep to these rules, and one draw needn't show every extreme that they name: `dest_patch`: within the 54 rows of one device (an aligned block of rows), no patch is named more than 14 times. `patch_home`: each position once.
All inputs are finite; a program needn't handle non-finite values.
Results may differ from the reference program's by a relative error of at most 0.0082.
Values may be sent and summed in bfloat16 or wider, within the bound.
No kernel may reach another device: no remote copies, remote signals or barrier semaphores. Data moves between devices by JAX's collectives and lax.ppermute only.
A program may use at most 128 MiB of HBM per device.

```python
import math
import jax
import jax.numpy as jnp
import numpy as np
from jax import lax

VISITS = 3
SIDE = 384
TILE = 128
KERNELS = 21
REACH = 10
LEVELS = 8
NDET = 48
TILES = 3
PIECES_DEV = 54
PIECES = 432
PATCHES = 8
CAP = 14


def set_ends(array, own_key, low, top_value):
    index_at = [jax.random.randint(jax.random.fold_in(own_key, axis), (), 0, length) for axis, length in enumerate(array.shape)]
    main_axis = array.shape.index(max(array.shape))
    next_to = index_at[:main_axis] + [(index_at[main_axis] + 1) % array.shape[main_axis]] + index_at[main_axis + 1:]
    return array.at[tuple(index_at)].set(low).at[tuple(next_to)].set(top_value)


def block_levels(stream_key, extent, cuts, smallest, largest):
    gain = 1.0
    for axis_at, parts in cuts:
        heights = jax.random.uniform(jax.random.fold_in(jax.random.fold_in(stream_key, 6), axis_at), (parts,), jnp.float32, smallest / len(cuts), largest / len(cuts))
        gain = gain * jnp.repeat(jnp.exp(heights), extent[axis_at] // parts).reshape((-1,) + (1,) * (len(extent) - 1 - axis_at))
    return gain


def routed_block(rng, own, number, rows, count, top, most, skew):
    order = jax.random.permutation(rng, count)
    crowded, common = portions_of(count, rows * top, most, skew, True), portions_of(count, rows * top, most, skew, False)
    places = jnp.arange(count)

    def named(lengths, rotation):
        used = int((lengths > 0).sum())
        fixed = max(1, used // 4)
        passed = fixed + (places - fixed + rotation * (used - fixed)) % max(1, count - fixed)
        return jnp.zeros((count,), jnp.int32).at[order[jnp.where(places < fixed, places, passed)]].set(jnp.asarray(lengths, jnp.int32))

    lengths = jnp.where(number % 4 == 0, named(crowded, number // 4), named(common, number - number // 4 - 1))
    mixed = jax.random.permutation(jax.random.fold_in(own, 3), count)
    giver, sink = mixed[0:count // 2 * 2:2], mixed[1:count // 2 * 2:2]
    margin = jnp.minimum(lengths[giver] - 1, most - lengths[sink]) // 2
    margin = jnp.where((giver == order[0]) | (sink == order[0]) | (lengths[sink] == 0), 0, jnp.maximum(margin, 0))
    passed = jax.random.randint(jax.random.fold_in(own, 4), (count // 2,), 0, 1 << 20) % (margin + 1)
    lengths = lengths.at[giver].add(-passed).at[sink].add(passed)
    items = jnp.searchsorted(jnp.cumsum(lengths), jnp.arange(rows * top), side="right").astype(jnp.int32)
    grid = items.reshape(top, rows).T
    grid = grid[jax.random.permutation(jax.random.fold_in(own, 1), rows)]
    rotation = jax.random.randint(jax.random.fold_in(own, 2), (rows, 1), 0, top)
    return jnp.take_along_axis(grid, (jnp.arange(top)[None, :] + rotation) % top, axis=1)


def portions_of(amount, total, limit, lean, full):
    portions = [(1 << 20) // math.isqrt(rank ** lean) + 1 for rank in range(1, amount + 1)]
    largest = limit if full else min(limit, max(-(-total // amount), total * portions[0] // sum(portions)))
    least = 1 if total - largest >= amount - 1 else 0
    holding, rest = [largest] + [least] * (amount - 1), total - largest - least * (amount - 1)
    while rest > 0:
        candidates = [i for i in range(1, amount) if holding[i] < largest] or [i for i in range(1, amount) if holding[i] < limit]
        mass, remaining = sum([portions[i] for i in candidates]), rest
        for i in candidates:
            more = min(limit - holding[i], max(1, remaining * portions[i] // mass), rest)
            holding[i] = holding[i] + more
            rest = rest - more
    return np.array(holding)


def gaussian(own_key, shape, deviation, most, cuts=(), dtype=jnp.bfloat16):
    result = jax.random.normal(own_key, shape, jnp.float32) * deviation
    if len(cuts) > 0:
        result = block_levels(own_key, shape, cuts, -0.22, 0.18) * result
    return jnp.clip(result, min=-most, max=most).astype(dtype)


def setup_inputs(seed: int = 0) -> dict:
    keys = jax.random.split(jax.random.key(seed), 11)
    images = gaussian(keys[0], (NDET, VISITS, SIDE, SIDE), 1.0, 6.0, ((0, 8), (2, 4)))
    warp_rows = gaussian(keys[1], (NDET, VISITS, SIDE, SIDE), SIDE ** -0.5, 0.3125, ((0, 8), (2, 4)))
    warp_cols = gaussian(keys[2], (NDET, VISITS, SIDE, SIDE), SIDE ** -0.5, 0.3125, ((0, 8),))
    psf_coef = gaussian(keys[3], (NDET, VISITS, KERNELS), KERNELS ** -0.5, 1.25, ((0, 8),), jnp.float32)
    taps = gaussian(keys[4], (KERNELS, 2 * REACH + 1), (2 * REACH + 1) ** -0.5, 1.25, (), jnp.float32)
    dest_patch_keys = jax.random.split(jax.random.fold_in(keys[5], 1), PIECES // PIECES_DEV)
    dest_patch_turns = jax.random.permutation(jax.random.fold_in(keys[5], 3), PIECES // PIECES_DEV)
    dest_patch = jax.vmap(lambda own, number: routed_block(jax.random.fold_in(keys[5], 2), own, number, PIECES_DEV, PATCHES, 1, CAP, 2))(dest_patch_keys, dest_patch_turns).reshape((PIECES, 1))
    dest_block = set_ends(jax.random.randint(keys[6], (PIECES,), 0, TILES), jax.random.fold_in(keys[6], 1), 0, TILES - 1).astype(jnp.int32)
    weight_index = set_ends(jax.random.randint(keys[7], (NDET, VISITS), 0, LEVELS), jax.random.fold_in(keys[7], 1), 0, LEVELS - 1).astype(jnp.int32)
    weight_table = jnp.clip(jnp.exp(jax.random.uniform(keys[8], (LEVELS,), jnp.float32, math.log(0.25), math.log(4.0))), 0.25, 4.0)
    patch_home = jax.random.permutation(keys[9], PATCHES).astype(jnp.int32)
    return {"images": images, "warp_rows": warp_rows, "warp_cols": warp_cols, "psf_coef": psf_coef, "taps": taps, "dest_patch": dest_patch, "dest_block": dest_block, "weight_index": weight_index, "weight_table": weight_table, "patch_home": patch_home}


def rounded(value):
    return lax.optimization_barrier(value.astype(jnp.bfloat16)).astype(jnp.float32)


def correlate(signal, kernel):
    reach = (kernel.shape[2] - 1) // 2
    return lax.conv_general_dilated(signal, kernel, (1,), [(reach, reach)], precision=lax.Precision.HIGHEST)


def reference(images, warp_rows, warp_cols, psf_coef, taps, dest_patch, dest_block, weight_index, weight_table, patch_home):
    taps_half = rounded(taps)

    def match_image(inputs):
        image, rows_map, cols_map, coef_row = inputs
        col_warped = jnp.dot(image, cols_map, preferred_element_type=jnp.float32).astype(jnp.bfloat16)
        warped = rounded(jnp.dot(rows_map, col_warped, preferred_element_type=jnp.float32))
        conv_cols = rounded(correlate(warped[:, None, :], taps_half[:, None, :]))
        scaled = rounded(coef_row[:, None] * taps)
        conv_rows = correlate(jnp.transpose(conv_cols, (2, 1, 0)), scaled[None])
        return jnp.transpose(conv_rows[:, 0, :])

    image_count = NDET * VISITS
    matched = lax.map(match_image, (images.reshape(image_count, SIDE, SIDE), warp_rows.reshape(image_count, SIDE, SIDE), warp_cols.reshape(image_count, SIDE, SIDE), psf_coef.reshape(image_count, KERNELS)))
    weights = weight_table[weight_index].reshape(image_count)
    weighted = rounded(weights[:, None, None] * matched)
    pieces = weighted.reshape(image_count, SIDE, TILES, TILE).transpose(0, 2, 1, 3).reshape(PIECES, SIDE, TILE)
    segment_ids = (patch_home[dest_patch[:, 0]] * TILES + dest_block).astype(jnp.int32)
    numerator = jax.ops.segment_sum(pieces, segment_ids, num_segments=PATCHES * TILES)
    denominator = jax.ops.segment_sum(jnp.repeat(weights, TILES), segment_ids, num_segments=PATCHES * TILES)
    template = rounded(numerator / jnp.maximum(denominator, 1.0)[:, None, None])
    coadd = template.reshape(PATCHES, TILES, SIDE, TILE).transpose(0, 2, 1, 3).reshape(PATCHES, SIDE, SIDE).astype(jnp.bfloat16)
    local_template = template[segment_ids].reshape(image_count, TILES, SIDE, TILE).transpose(0, 2, 1, 3).reshape(image_count, SIDE, SIDE)
    difference = (matched - local_template).astype(jnp.bfloat16).reshape(NDET, VISITS, SIDE, SIDE)
    return difference, coadd
```

```python
import functools

import jax
import jax.numpy as jnp
from jax import lax
from jax.experimental import pallas as pl
from jax.experimental.pallas import tpu as pltpu
from jax.sharding import PartitionSpec as P

TILE = 128
ALIGN = 16
CHUNKS = (6, 6, 3, 3)
VMEM = 56 * 1024 * 1024
F32 = jnp.float32
BF16 = jnp.bfloat16


def match_kernel(
    slot_ref,
    weight_ref,
    row_ref,
    *refs,
    start,
    taps,
    shards,
    first,
    last,
    parts,
):
    shard_refs = refs[:shards]
    rows_ref, above_ref, below_ref, cols_ref, profile_ref = refs[shards : shards + 5]
    refs = refs[shards + 5 :]
    if not first:
        numer_in = refs[1]
        refs = refs[2:]
    matched_ref = refs[0]
    if last:
        part_refs = refs[1 : 1 + parts]
        numer = refs[1 + parts]
        refs = refs[2 + parts :]
    else:
        numer = refs[1]
        refs = refs[2:]
    image, extended, wide, stack, table = refs
    step = pl.program_id(0)
    band, side = rows_ref.shape[1:]
    pad = above_ref.shape[1]
    span = band + 2 * pad
    reach = (taps - 1) // 2
    tiles = side // TILE

    @pl.when(step == 0)
    def _():
        wide[...] = jnp.zeros_like(wide)
        if first:
            numer[...] = jnp.zeros_like(numer)
        else:
            numer[...] = numer_in[...]

    row = row_ref[0]
    for mask, shard in enumerate(shard_refs):
        at = pl.multiple_of((row ^ mask) * band, band)
        image[pl.ds(at, band), :] = shard[0]
    extended[0:pad, :] = above_ref[0]
    extended[pad : pad + band, :] = rows_ref[0]
    extended[pad + band : span, :] = below_ref[0]
    by_rows = jnp.dot(extended[...], image[...], preferred_element_type=F32).astype(BF16)
    warped = jnp.dot(by_rows, cols_ref[0], preferred_element_type=F32).astype(BF16)
    wide[:, TILE : TILE + side] = warped
    for t in range(taps):
        left = TILE - reach + t
        stack[span * t : span * (t + 1), :] = wide[:, left : left + side]
        profile = jnp.broadcast_to(profile_ref[0, t : t + 1, :], (band, span))
        shifted = pltpu.roll(profile, 0, 1, stride=1, stride_axis=0)
        table[:, span * t : span * (t + 1)] = shifted.astype(BF16)
    matched = jnp.dot(table[...], stack[...], preferred_element_type=F32)
    matched_ref[0] = matched
    index = start + step
    weight = weight_ref[index]
    for q in range(tiles):
        slot = slot_ref[index * tiles + q]
        piece = (weight * matched[:, TILE * q : TILE * (q + 1)]).astype(BF16)
        numer[slot] += piece.astype(F32)

    if last:

        @pl.when(step == pl.num_programs(0) - 1)
        def _():
            each = numer.shape[0] // parts
            for m in range(parts):
                part_refs[m][...] = numer[each * m : each * (m + 1)].astype(BF16)


def match_chunk(slots, weights, row, shards, operands, carry, start, count, taps, parts, last):
    rows, above, below, cols, profiles = operands
    images, band, side = rows.shape
    pad = above.shape[1]
    span = band + 2 * pad
    slot_count = parts * (side // TILE)
    first = carry is None

    def per_image(array):
        offset = start if array.shape[0] == images else 0
        return pl.BlockSpec((1,) + array.shape[1:], lambda i, *_: (i + offset, 0, 0))

    def whole(shape):
        return pl.BlockSpec(shape, lambda i, *_: (0,) * len(shape))

    arrays = list(shards) + [rows, above, below, cols, profiles]
    in_specs = [per_image(a) for a in arrays]
    aliases = {}
    numer_shape = (slot_count, band, TILE)
    if not first:
        aliases = {3 + len(arrays): 0}
        arrays += list(carry)
        in_specs += [pl.BlockSpec(memory_space=pl.ANY), whole(numer_shape)]
    out_shape = [jax.ShapeDtypeStruct((images, band, side), F32)]
    out_specs = [pl.BlockSpec((1, band, side), lambda i, *_: (i + start, 0, 0))]
    scratch = []
    if last:
        part = (slot_count // parts, band, TILE)
        out_shape += [jax.ShapeDtypeStruct(part, BF16)] * parts
        out_specs += [whole(part)] * parts
        scratch = [pltpu.VMEM(numer_shape, F32)]
    else:
        out_shape.append(jax.ShapeDtypeStruct(numer_shape, F32))
        out_specs.append(whole(numer_shape))
    scratch += [
        pltpu.VMEM((side, side), BF16),
        pltpu.VMEM((span, side), BF16),
        pltpu.VMEM((span, side + 2 * TILE), BF16),
        pltpu.VMEM((taps * span, side), BF16),
        pltpu.VMEM((band, taps * span), BF16),
    ]
    flops = 2 * count * (2 * span * side * side + band * taps * span * side)
    return pl.pallas_call(
        functools.partial(
            match_kernel,
            start=start,
            taps=taps,
            shards=len(shards),
            first=first,
            last=last,
            parts=parts,
        ),
        grid_spec=pltpu.PrefetchScalarGridSpec(
            num_scalar_prefetch=3,
            grid=(count,),
            in_specs=in_specs,
            out_specs=out_specs,
            scratch_shapes=scratch,
        ),
        out_shape=out_shape,
        input_output_aliases=aliases,
        compiler_params=pltpu.CompilerParams(vmem_limit_bytes=VMEM),
        cost_estimate=pl.CostEstimate(
            flops=flops, bytes_accessed=count * 900000, transcendentals=0
        ),
    )(slots, weights, row, *arrays)


def template_kernel(denom_ref, *refs):
    part_refs, template_ref, coadd_ref = refs[:-2], refs[-2], refs[-1]
    for q in range(template_ref.shape[0]):
        total = part_refs[0][q].astype(F32)
        for part in part_refs[1:]:
            total = total + part[q].astype(F32)
        box = (total / jnp.maximum(denom_ref[q], 1.0)).astype(BF16)
        template_ref[q] = box
        coadd_ref[:, TILE * q : TILE * (q + 1)] = box


def difference_kernel(slot_ref, matched_ref, *refs):
    template_refs, out_ref, held = refs[:-2], refs[-2], refs[-1]
    step = pl.program_id(0)
    each = template_refs[0].shape[0]
    count, _, side = matched_ref.shape
    tiles = side // TILE

    @pl.when(step == 0)
    def _():
        for m, template in enumerate(template_refs):
            held[each * m : each * (m + 1)] = template[...]

    for i in range(count):
        for q in range(tiles):
            slot = slot_ref[(step * count + i) * tiles + q]
            columns = slice(TILE * q, TILE * (q + 1))
            box = held[slot].astype(F32)
            out_ref[i, :, columns] = (matched_ref[i, :, columns] - box).astype(BF16)


def exchange(value, axis, mask):
    size = lax.axis_size(axis)
    return lax.ppermute(value, axis, [(i, i ^ mask) for i in range(size)])


def per_device(
    images,
    warp_rows,
    warp_cols,
    psf_coef,
    taps,
    dest_patch,
    dest_block,
    weight_index,
    weight_table,
    patch_home,
):
    det_count, visit_count, band, side = images.shape
    kernel_count, tap_count = taps.shape
    reach = (tap_count - 1) // 2
    pad = -(-reach // ALIGN) * ALIGN
    span = band + 2 * pad
    tiles = side // TILE
    det_devices = lax.axis_size("det")
    row_devices = lax.axis_size("row")
    mine = lax.axis_index("det")
    row = lax.axis_index("row").astype(jnp.int32).reshape(1)
    image_count = det_count * visit_count
    pixels = images.reshape(image_count, band, side)
    rows = warp_rows.reshape(image_count, band, side)
    cols = warp_cols.reshape(image_count, side, side)

    chunks = CHUNKS if sum(CHUNKS) == image_count else (image_count,)
    starts = [sum(chunks[:c]) for c in range(len(chunks))]
    far = [exchange(pixels[s : s + n], "row", 2) for s, n in zip(starts, chunks)]
    sibling = exchange(pixels, "row", 1)
    upward = [(i, i + 1) for i in range(row_devices - 1)]
    downward = [(j, i) for i, j in upward]
    above = lax.ppermute(rows[:, band - pad :], "row", upward)
    below = lax.ppermute(rows[:, :pad], "row", downward)

    with jax.named_scope("profiles"):
        scaled = (psf_coef.reshape(image_count, kernel_count)[:, :, None] * taps).astype(BF16)
        profiles = jnp.einsum(
            "nkt,ku->nut", scaled, taps.astype(BF16), preferred_element_type=F32
        )
        profiles = jnp.pad(
            profiles,
            ((0, 0), (0, -tap_count % 8), (pad - reach, span - tap_count - pad + reach)),
        )
    with jax.named_scope("targets"):
        level_count = weight_table.shape[0]
        levels = jnp.arange(level_count)
        weight_all = jnp.sum(
            jnp.where(weight_index[:, :, None] == levels, weight_table, 0.0), axis=2
        ).reshape(-1)
        weights = lax.dynamic_slice_in_dim(weight_all, mine * image_count, image_count, 0)
        patches = jnp.arange(patch_home.shape[0])
        owner = jnp.sum(jnp.where(dest_patch == patches, patch_home, 0), axis=1)
        slot_all = (owner ^ mine) * tiles + dest_block
        slots = lax.dynamic_slice_in_dim(
            slot_all, mine * image_count * tiles, image_count * tiles, 0
        )
        piece_weight = jnp.repeat(weight_all, tiles)
        own = slot_all[:, None] == jnp.arange(tiles)
        denom = jnp.sum(jnp.where(own, piece_weight[:, None], 0.0), axis=0)

    carry = None
    for c, (s, n) in enumerate(zip(starts, chunks)):
        diagonal = exchange(far[c], "row", 1)
        shards = (pixels, sibling, far[c], diagonal)
        carry = match_chunk(
            slots,
            weights,
            row,
            shards,
            (rows, above, below, cols, profiles),
            carry,
            s,
            n,
            tap_count,
            det_devices,
            c == len(chunks) - 1,
        )
    matched, parts = carry[0], carry[1:]
    received = [parts[0]] + [exchange(parts[m], "det", m) for m in range(1, det_devices)]
    box_shape = (tiles, band, TILE)
    template, coadd = pl.pallas_call(
        template_kernel,
        in_specs=[pl.BlockSpec(memory_space=pltpu.SMEM)]
        + [pl.BlockSpec(memory_space=pltpu.VMEM)] * det_devices,
        out_specs=[pl.BlockSpec(memory_space=pltpu.VMEM)] * 2,
        out_shape=[
            jax.ShapeDtypeStruct(box_shape, BF16),
            jax.ShapeDtypeStruct((band, side), BF16),
        ],
        compiler_params=pltpu.CompilerParams(vmem_limit_bytes=VMEM),
    )(denom, *received)
    templates = [template] + [exchange(template, "det", m) for m in range(1, det_devices)]
    group = 3 if image_count % 3 == 0 else 1
    block = pl.BlockSpec((group, band, side), lambda i, *_: (i, 0, 0))
    difference = pl.pallas_call(
        difference_kernel,
        grid_spec=pltpu.PrefetchScalarGridSpec(
            num_scalar_prefetch=1,
            grid=(image_count // group,),
            in_specs=[block] + [pl.BlockSpec(box_shape, lambda i, *_: (0, 0, 0))] * det_devices,
            out_specs=block,
            scratch_shapes=[pltpu.VMEM((det_devices * tiles, band, TILE), BF16)],
        ),
        out_shape=jax.ShapeDtypeStruct((image_count, band, side), BF16),
        compiler_params=pltpu.CompilerParams(vmem_limit_bytes=VMEM),
    )(slots, matched, *templates)
    return difference.reshape(images.shape), coadd.reshape(1, band, side)


def solution(mesh):
    placed = (
        P("det", None, "row", None),
        P("det", None, "row", None),
        P("det", None, None, None),
        P("det", None, None),
        P(),
        P(),
        P(),
        P(),
        P(),
        P(),
    )
    return jax.shard_map(
        per_device,
        mesh=mesh,
        in_specs=placed,
        out_specs=(P("det", None, "row", None), P("det", "row", None)),
        check_vma=False,
    )
```

```python
import functools

import jax
import jax.numpy as jnp
from jax import lax
from jax.experimental import pallas as pl
from jax.experimental.pallas import tpu as pltpu
from jax.sharding import PartitionSpec as P

TILE = 128
ALIGN = 16
CHUNKS = (4, 3, 2)
INNER = 7
MIB = 1024 * 1024
F32 = jnp.float32
BF16 = jnp.bfloat16


def match_kernel(
    slot_ref, weight_ref, row_ref, *refs, start, taps, first, last
):
    shard_refs = refs[:4]
    rows_refs = refs[4:6]
    edge_refs = refs[6:8]
    cols_ref, profile_ref = refs[8:10]
    refs = refs[10:]
    if not first:
        carried = refs[2:4]
        refs = refs[4:]
    matched_refs, sums_refs = refs[:2], refs[2:4]
    refs = refs[4:]
    image, extended, wide, stack, table = refs[:5]
    numers = (sums_refs[0], refs[5]) if last else sums_refs
    step = pl.program_id(0)
    images = pl.num_programs(0)
    band, side = rows_refs[0].shape[1:]
    pad = edge_refs[0].shape[1]
    span = band + 2 * pad
    reach = (taps - 1) // 2
    outer = -(-taps // INNER)
    tiles = side // TILE
    width = stack.shape[2]
    row = row_ref[0]
    core = row & 1

    @pl.when(step == 0)
    def _():
        wide[...] = jnp.zeros_like(wide)
        table[...] = jnp.zeros_like(table)
        for m in range(2):
            numers[m][...] = jnp.zeros_like(numers[m]) if first else carried[m][...]

    for mask, shard in enumerate(shard_refs):
        at = pl.multiple_of((row ^ mask) * band, band)
        image[pl.ds(at, band), :] = shard[0]
    edge = edge_refs[0][0] + edge_refs[1][0]
    blank = jnp.zeros_like(edge)
    extended[0:pad, :] = jnp.where(row >= 2, edge, blank)
    extended[pad + 2 * band :, :] = jnp.where(row >= 2, blank, edge)
    for m, rows in enumerate(rows_refs):
        at = pl.multiple_of(pad + (core ^ m) * band, ALIGN)
        extended[pl.ds(at, band), :] = rows[0]
    by_rows = jnp.dot(extended[...], image[...], preferred_element_type=F32).astype(BF16)
    warped = jnp.dot(by_rows, cols_ref[0], preferred_element_type=F32).astype(BF16)
    wide[:, TILE : TILE + side] = warped
    for b in range(INNER):
        left = TILE - reach + b
        shifted = wide[:, left : left + width]
        for half in range(2):
            stack[half, span * b : span * (b + 1), :] = shifted[band * half : band * half + span]
    for t in range(taps):
        a, b = t // INNER, t % INNER
        profile = jnp.broadcast_to(profile_ref[0, t : t + 1, :], (band, span))
        toeplitz = pltpu.roll(profile, 0, 1, stride=1, stride_axis=0).astype(BF16)
        table[band * a : band * (a + 1), span * b : span * (b + 1)] = toeplitz
    index = start + step
    weight = weight_ref[index]
    for m in range(2):
        partial = jnp.dot(table[...], stack[core ^ m], preferred_element_type=F32)
        matched = partial[0:band, 0:side]
        for a in range(1, outer):
            matched = matched + partial[band * a : band * (a + 1), INNER * a : INNER * a + side]
        matched_refs[m][0] = matched
        for q in range(tiles):
            slot = slot_ref[index * tiles + q]
            piece = (weight * matched[:, TILE * q : TILE * (q + 1)]).astype(BF16)
            numers[m][slot] += piece.astype(F32)

    if last:

        @pl.when(step == images - 1)
        def _():
            sums_refs[1][...] = numers[1][...].astype(BF16)


def match_chunk(slots, weights, row, operands, carry, start, count, taps, slot_count, last):
    pixels, _, _, _, rows, _, edge, _, _, _ = operands
    images, band, side = pixels.shape
    half = images // 2
    pad = edge.shape[1]
    span = band + 2 * pad
    outer = -(-taps // INNER)
    first = carry is None
    width = side + TILE

    def block(array):
        if array.shape[0] == images:
            place = lambda i, slot, weight, row: ((row[0] & 1) * half + start + i, 0, 0)
        elif array.shape[0] == half:
            place = lambda i, *_: (start + i, 0, 0)
        else:
            place = lambda i, *_: (i, 0, 0)
        return pl.BlockSpec((1,) + array.shape[1:], place)

    whole = lambda shape: pl.BlockSpec(shape, lambda i, *_: (0,) * len(shape))
    in_specs = [block(a) for a in operands]
    arrays = [
        pltpu.with_memory_space_constraint(a, pltpu.HBM) if a.shape[0] == images else a
        for a in operands
    ]
    aliases = {}
    numer_shape = (slot_count, band, TILE)
    matched_shape = jax.ShapeDtypeStruct((half, band, side), F32)
    if not first:
        aliases = {3 + len(arrays): 0, 4 + len(arrays): 1}
        arrays += list(carry)
        in_specs += [pl.BlockSpec(memory_space=pl.ANY)] * 2 + [whole(numer_shape)] * 2
    out_shape = [matched_shape] * 2 + [
        jax.ShapeDtypeStruct(numer_shape, F32),
        jax.ShapeDtypeStruct(numer_shape, BF16 if last else F32),
    ]
    out_specs = [block(matched_shape)] * 2 + [whole(numer_shape)] * 2
    scratch = [
        pltpu.VMEM((side, side), BF16),
        pltpu.VMEM((2 * band + 2 * pad, side), BF16),
        pltpu.VMEM((2 * band + 2 * pad, side + 3 * TILE), BF16),
        pltpu.VMEM((2, INNER * span, width), BF16),
        pltpu.VMEM((outer * band, INNER * span), BF16),
    ]
    if last:
        scratch.append(pltpu.VMEM(numer_shape, F32))
    numer_bytes = 4 * slot_count * band * TILE
    return pl.pallas_call(
        functools.partial(match_kernel, start=start, taps=taps, first=first, last=last),
        grid_spec=pltpu.PrefetchScalarGridSpec(
            num_scalar_prefetch=3,
            grid=(count,),
            in_specs=in_specs,
            out_specs=out_specs,
            scratch_shapes=scratch,
        ),
        out_shape=out_shape,
        input_output_aliases=aliases,
        compiler_params=pltpu.CompilerParams(
            vmem_limit_bytes=min(60 * MIB, 36 * MIB + (4 if first else 8) * numer_bytes)
        ),
        cost_estimate=pl.CostEstimate(
            flops=count * 2000000000, bytes_accessed=count * 1000000, transcendentals=0
        ),
    )(slots, weights, row, *arrays)


def merge_kernel(own_ref, other_ref, *part_refs):
    each = part_refs[0].shape[0]
    for m, part in enumerate(part_refs):
        boxes = slice(each * m, each * (m + 1))
        part[...] = (own_ref[boxes] + other_ref[boxes].astype(F32)).astype(BF16)


def template_kernel(denom_ref, *refs):
    part_refs, template_ref, coadd_ref = refs[:-2], refs[-2], refs[-1]
    for q in range(template_ref.shape[0]):
        total = part_refs[0][q].astype(F32)
        for part in part_refs[1:]:
            total = total + part[q].astype(F32)
        box = (total / jnp.maximum(denom_ref[q], 1.0)).astype(BF16)
        template_ref[q] = box
        coadd_ref[:, TILE * q : TILE * (q + 1)] = box


def difference_kernel(slot_ref, row_ref, own_ref, other_ref, *refs):
    template_refs, out_ref, held = refs[:-2], refs[-2], refs[-1]
    step = pl.program_id(0)
    each = template_refs[0].shape[0]
    count, _, side = own_ref.shape
    tiles = side // TILE

    @pl.when(step == 0)
    def _():
        for m, template in enumerate(template_refs):
            held[each * m : each * (m + 1)] = template[...]

    def subtract(matched_ref):
        for i in range(count):
            for q in range(tiles):
                slot = slot_ref[(step * count + i) * tiles + q]
                columns = slice(TILE * q, TILE * (q + 1))
                box = held[slot].astype(F32)
                out_ref[i, :, columns] = (matched_ref[i, :, columns] - box).astype(BF16)

    mine = (step * 2 // pl.num_programs(0)) == (row_ref[0] & 1)
    pl.when(mine)(lambda: subtract(own_ref))
    pl.when(jnp.logical_not(mine))(lambda: subtract(other_ref))


def exchange(value, axis, mask, turn=0):
    size = lax.axis_size(axis)
    pairs = [(i, i ^ mask) for i in range(size)]
    return lax.ppermute(value, axis, pairs[turn:] + pairs[:turn])


def per_device(
    images,
    warp_rows,
    warp_cols,
    psf_coef,
    taps,
    dest_patch,
    dest_block,
    weight_index,
    weight_table,
    patch_home,
):
    det_count, visit_count, band, side = images.shape
    kernel_count, tap_count = taps.shape
    reach = (tap_count - 1) // 2
    pad = -(-reach // ALIGN) * ALIGN
    span = band + 2 * pad
    tiles = side // TILE
    det_devices = lax.axis_size("det")
    mine = lax.axis_index("det")
    row = lax.axis_index("row").astype(jnp.int32)
    core = row & 1
    image_count = det_count * visit_count
    half = image_count // 2
    assert lax.axis_size("row") == 4 and image_count == 2 * half
    pixels = images.reshape(image_count, band, side)
    rows = warp_rows.reshape(image_count, band, side)
    cols = warp_cols.reshape(image_count, side, side)
    row_one = row.reshape(1)

    chunks = CHUNKS if sum(CHUNKS) == half and det_devices <= 8 else (half,)
    starts = [sum(chunks[:c]) for c in range(len(chunks))]

    def portion(array, which, first, count):
        return lax.dynamic_slice_in_dim(array, (core ^ which) * half + first, count, 0)

    far, cross = [], []
    for c, (s, n) in enumerate(zip(starts, chunks)):
        far.append(exchange(portion(pixels, 0, s, n), "row", 2, c))
        cross.append(exchange(portion(pixels, 1, s, n), "row", 3, c))
    sibling = exchange(portion(pixels, 1, 0, half), "row", 1)
    sibling_rows = exchange(portion(rows, 1, 0, half), "row", 1)
    edge_at = jnp.where(row < 2, band - pad, 0)

    def edge(which, pairs):
        part = lax.dynamic_slice(
            rows, ((core ^ which) * half, edge_at, 0), (half, pad, side)
        )
        return lax.ppermute(part, "row", pairs)

    edges = (edge(0, [(2, 0), (1, 3)]), edge(1, [(2, 1), (1, 2)]))

    with jax.named_scope("profiles"):
        scaled = (psf_coef.reshape(image_count, kernel_count)[:, :, None] * taps).astype(BF16)
        profiles = jnp.einsum(
            "nkt,ku->nut", scaled, taps.astype(BF16), preferred_element_type=F32
        )
        profiles = jnp.pad(
            profiles,
            ((0, 0), (0, -tap_count % 8), (pad - reach, span - tap_count - pad + reach)),
        )
    with jax.named_scope("targets"):
        levels = jnp.arange(weight_table.shape[0])
        weight_all = jnp.sum(
            jnp.where(weight_index[:, :, None] == levels, weight_table, 0.0), axis=2
        ).reshape(-1)
        weights = lax.dynamic_slice_in_dim(weight_all, mine * image_count + core * half, half, 0)
        patches = jnp.arange(patch_home.shape[0])
        owner = jnp.sum(jnp.where(dest_patch == patches, patch_home, 0), axis=1)
        slot_all = (owner ^ mine) * tiles + dest_block
        slots = lax.dynamic_slice_in_dim(
            slot_all, mine * image_count * tiles, image_count * tiles, 0
        )
        own_slots = lax.dynamic_slice_in_dim(slots, core * half * tiles, half * tiles, 0)
        piece_weight = jnp.repeat(weight_all, tiles)
        own = slot_all[:, None] == jnp.arange(tiles)
        denom = jnp.sum(jnp.where(own, piece_weight[:, None], 0.0), axis=0)

    carry = None
    slot_count = det_devices * tiles
    for c, (s, n) in enumerate(zip(starts, chunks)):
        operands = (
            pixels, sibling, far[c], cross[c], rows, sibling_rows, edges[0], edges[1], cols, profiles,
        )
        carry = match_chunk(
            own_slots, weights, row_one, operands, carry, s, n, tap_count, slot_count,
            c == len(chunks) - 1,
        )
    matched, matched_sent, own_sums, sums_sent = carry
    other_sums = exchange(sums_sent, "row", 1)
    box_shape = (tiles, band, TILE)
    box = jax.ShapeDtypeStruct(box_shape, BF16)
    in_vmem = pl.BlockSpec(memory_space=pltpu.VMEM)
    small = pltpu.CompilerParams(vmem_limit_bytes=4 * MIB + 16 * slot_count * band * TILE)
    parts = pl.pallas_call(
        merge_kernel,
        in_specs=[in_vmem] * 2,
        out_specs=[in_vmem] * det_devices,
        out_shape=[box] * det_devices,
        compiler_params=small,
    )(own_sums, other_sums)
    order = sorted(range(1, det_devices), key=lambda m: -m)
    received = [parts[0]] + [None] * (det_devices - 1)
    for m in order:
        received[m] = exchange(parts[m], "det", m)
    other_matched = exchange(matched_sent, "row", 1)
    template, coadd = pl.pallas_call(
        template_kernel,
        in_specs=[pl.BlockSpec(memory_space=pltpu.SMEM)] + [in_vmem] * det_devices,
        out_specs=[in_vmem] * 2,
        out_shape=[box, jax.ShapeDtypeStruct((band, side), BF16)],
        compiler_params=small,
    )(denom, *received)
    templates = [template] + [None] * (det_devices - 1)
    for m in order:
        templates[m] = exchange(template, "det", m)
    group = 3 if half % 3 == 0 else 1
    steps = half // group

    def half_block(which):
        def place(i, slot, row):
            return (jnp.clip(i - ((row[0] & 1) ^ which) * steps, 0, steps - 1), 0, 0)

        return pl.BlockSpec((group, band, side), place)

    difference = pl.pallas_call(
        difference_kernel,
        grid_spec=pltpu.PrefetchScalarGridSpec(
            num_scalar_prefetch=2,
            grid=(2 * steps,),
            in_specs=[half_block(0), half_block(1)]
            + [pl.BlockSpec(box_shape, lambda i, *_: (0, 0, 0))] * det_devices,
            out_specs=pl.BlockSpec((group, band, side), lambda i, *_: (i, 0, 0)),
            scratch_shapes=[pltpu.VMEM((slot_count, band, TILE), BF16)],
        ),
        out_shape=jax.ShapeDtypeStruct((image_count, band, side), BF16),
        compiler_params=small,
    )(slots, row_one, matched, other_matched, *templates)
    return difference.reshape(images.shape), coadd.reshape(1, band, side)


def solution(mesh):
    placed = (
        P("det", None, "row", None),
        P("det", None, "row", None),
        P("det", None, None, None),
        P("det", None, None),
        P(),
        P(),
        P(),
        P(),
        P(),
        P(),
    )
    return jax.shard_map(
        per_device,
        mesh=mesh,
        in_specs=placed,
        out_specs=(P("det", None, "row", None), P("det", "row", None)),
        check_vma=False,
    )
```

```python
import functools

import jax
import jax.numpy as jnp
from jax import lax
from jax.experimental import pallas as pl
from jax.experimental.pallas import tpu as pltpu
from jax.sharding import PartitionSpec as P

TILE = 128
ALIGN = 16
CHUNKS = (4, 3, 2)
BLOCK = 48
DEPTH = 256
MIB = 1024 * 1024
VMEM = 44 * MIB
F32 = jnp.float32
BF16 = jnp.bfloat16


def pack_kernel(row_ref, *refs, chunks, siblings, edges):
    count = 2 * len(chunks) + 2 * siblings + edges
    sems = refs[-1]
    outs, held = refs[-1 - 2 * count : -1 - count], refs[-1 - count : -1]
    pixels_ref, rows_ref = refs[:2]
    half = pixels_ref.shape[0] // 2
    row = row_ref[0]
    core = row & 1
    pieces = []
    if siblings:
        other = pl.ds((1 - core) * half, half)
        pieces += [rows_ref.at[other], pixels_ref.at[other]]
    for s, n in chunks:
        for which in range(2):
            pieces.append(pixels_ref.at[pl.ds((core ^ which) * half + s, n)])
    fetches = [
        pltpu.make_async_copy(piece, kept, sems.at[0, i])
        for i, (piece, kept) in enumerate(zip(pieces, held))
    ]
    stores = [
        pltpu.make_async_copy(kept, out, sems.at[1, i])
        for i, (kept, out) in enumerate(zip(held, outs))
    ]
    if edges:
        pad = outs[-1].shape[1]
        first = jnp.where(row < 2, rows_ref.shape[1] - pad, 0)
        near = pl.ds(pl.multiple_of(first, ALIGN), pad)
        holds = core == (row < 2).astype(jnp.int32)
        own = rows_ref.at[pl.ds(core * half, half), near]
        edge = pltpu.make_async_copy(own, held[-1], sems.at[0, count - 1])
        passed = pltpu.make_async_copy(refs[2].at[:, near], held[-1], sems.at[0, count - 1])
        pl.when(holds)(edge.start)
        pl.when(jnp.logical_not(holds))(passed.start)
        fetches.append(edge)
    for fetch in fetches[: len(pieces)]:
        fetch.start()
    for fetch, store in zip(fetches, stores):
        fetch.wait()
        store.start()
    for store in stores:
        store.wait()


def pack(row, pixels, rows, chunks, pad, siblings=False, sibling_rows=None, after=()):
    images, band, side = pixels.shape
    half = images // 2
    shapes = [(half, band, side)] * 2 if siblings else []
    shapes += [(n, band, side) for _, n in chunks for _ in range(2)]
    arrays = [pltpu.with_memory_space_constraint(a, pltpu.HBM) for a in (pixels, rows)]
    if sibling_rows is not None:
        shapes.append((half, pad, side))
        arrays.append(sibling_rows)
    arrays += after
    anywhere = pl.BlockSpec(memory_space=pl.ANY)
    return pl.pallas_call(
        functools.partial(
            pack_kernel, chunks=chunks, siblings=siblings, edges=sibling_rows is not None
        ),
        in_specs=[pl.BlockSpec(memory_space=pltpu.SMEM)] + [anywhere] * len(arrays),
        out_specs=[anywhere] * len(shapes),
        out_shape=[jax.ShapeDtypeStruct(shape, BF16) for shape in shapes],
        scratch_shapes=[pltpu.VMEM(shape, BF16) for shape in shapes]
        + [pltpu.SemaphoreType.DMA((2, len(shapes)))],
        compiler_params=pltpu.CompilerParams(vmem_limit_bytes=VMEM),
    )(row, *arrays)


def target_kernel(
    place_ref, patch_ref, block_ref, level_ref, table_ref, home_ref, _, slots_ref, own_ref, weights_ref, denom_ref, *, tiles
):
    mine, core = place_ref[0], place_ref[1] & 1
    visits, detectors = level_ref.shape
    pieces = slots_ref.shape[0]
    half = weights_ref.shape[0]
    first = mine * (half * 2)

    def slot_of(n):
        return (home_ref[patch_ref[n]] ^ mine) * tiles + block_ref[n]

    def place(i, _):
        slots_ref[i] = slot_of(mine * pieces + i)
        return 0

    def place_own(i, _):
        own_ref[i] = slots_ref[core * half * tiles + i]
        return 0

    def weigh(i, _):
        image = first + core * half + i
        weights_ref[i] = table_ref[level_ref[image % visits, image // visits]]
        return 0

    def add(d, sums):
        for v in range(visits):
            weight = table_ref[level_ref[v, d]]
            for q in range(tiles):
                slot = slot_of((d * visits + v) * tiles + q)
                sums = tuple(
                    total + jnp.where(slot == t, weight, 0.0) for t, total in enumerate(sums)
                )
        return sums

    lax.fori_loop(0, pieces, place, 0)
    lax.fori_loop(0, half * tiles, place_own, 0)
    lax.fori_loop(0, half, weigh, 0)
    sums = lax.fori_loop(0, detectors, add, (jnp.float32(0),) * tiles)
    for t in range(tiles):
        denom_ref[t] = sums[t]


def match_kernel(slot_ref, weight_ref, row_ref, *refs, start, taps, first, last):
    shard_refs = refs[:4]
    rows_refs = refs[4:6]
    edge_ref, cols_ref, profile_ref = refs[6:9]
    refs = refs[9:]
    if not first:
        carried = refs[2:4]
        refs = refs[4:]
    matched_refs, sums_refs = refs[:2], refs[2:4]
    refs = refs[4:]
    count, band, side = rows_refs[0].shape
    group = [refs[g : 4 * count : count] for g in range(count)]
    numers = (sums_refs[0], refs[4 * count]) if last else sums_refs
    pad = edge_ref.shape[1]
    span = BLOCK + 2 * pad
    reach = (taps - 1) // 2
    inner = DEPTH // span
    outer = -(-taps // inner)
    tiles = side // TILE
    width = side + TILE
    blocks = band // BLOCK
    row = row_ref[0]
    core = row & 1

    for m in range(2):
        numers[m][...] = jnp.zeros_like(numers[m]) if first else carried[m][...]
    for g in range(count):
        image, extended, stack, table = group[g]
        for mask, shard in enumerate(shard_refs):
            at = pl.multiple_of((row ^ mask) * band, band)
            image[pl.ds(at, band), :] = shard[g]
        edge = edge_ref[g]
        blank = jnp.zeros_like(edge)
        extended[0:pad, :] = jnp.where(row >= 2, edge, blank)
        extended[pad + 2 * band :, :] = jnp.where(row >= 2, blank, edge)
        for m, rows in enumerate(rows_refs):
            at = pl.multiple_of(pad + (core ^ m) * band, ALIGN)
            extended[pl.ds(at, band), :] = rows[g]
        by_rows = jnp.dot(extended[...], image[...], preferred_element_type=F32).astype(BF16)
        warped = jnp.dot(by_rows, cols_ref[g], preferred_element_type=F32).astype(BF16)
        ring = jnp.concatenate([warped, jnp.zeros((warped.shape[0], TILE), BF16)], axis=1)
        for b in range(inner):
            turn = (inner // 2 - b) % width
            shifted = pltpu.roll(ring, turn, 1) if turn else ring
            for k in range(2 * blocks):
                stack[k, span * b : span * (b + 1), :] = shifted[BLOCK * k : BLOCK * k + span]
        for k in range(2 * blocks):
            stack[k, span * inner :, :] = jnp.zeros((DEPTH - span * inner, width), BF16)
        profiles = None
        for b in range(inner):
            part = profile_ref[g, pl.ds(b, outer, stride=inner), :]
            part = jnp.concatenate([part, jnp.zeros((outer, DEPTH - TILE), F32)], axis=1)
            part = pltpu.roll(part, span * b, 1) if b else part
            profiles = part if profiles is None else profiles + part
        for a in range(outer):
            profile = jnp.broadcast_to(profiles[a : a + 1, :], (BLOCK, DEPTH))
            toeplitz = pltpu.roll(profile, 0, 1, stride=1, stride_axis=0)
            table[BLOCK * a : BLOCK * (a + 1), :] = toeplitz.astype(BF16)
    middle = outer // 2
    origin = inner * middle + inner // 2 - reach
    for g in range(count):
        _, _, stack, table = group[g]
        index = start + g
        weight = weight_ref[index]
        for m in range(2):
            for k in range(blocks):
                partial = jnp.dot(
                    table[...], stack[(core ^ m) * blocks + k], preferred_element_type=F32
                )
                total = None
                for a in range(outer):
                    turn = (inner * (middle - a) - origin) % width
                    part = partial[BLOCK * a : BLOCK * (a + 1)]
                    part = pltpu.roll(part, turn, 1) if turn else part
                    total = part if total is None else total + part
                matched = total[:, 0:side]
                here = slice(BLOCK * k, BLOCK * (k + 1))
                matched_refs[m][g, here, :] = matched
                for q in range(tiles):
                    slot = slot_ref[index * tiles + q]
                    piece = (weight * matched[:, TILE * q : TILE * (q + 1)]).astype(BF16)
                    numers[m][slot, here, :] += piece.astype(F32)
    if last:
        sums_refs[1][...] = numers[1][...].astype(BF16)


def match_chunk(slots, weights, row, operands, carry, start, count, taps, slot_count, last):
    pixels, rows, edge = operands[0], operands[4], operands[6]
    images, band, side = pixels.shape
    half = images // 2
    pad = edge.shape[1]
    inner = DEPTH // (BLOCK + 2 * pad)
    outer = -(-taps // inner)
    width = side + TILE
    first = carry is None

    def block(array):
        if array.shape[0] == images:
            place = lambda i, slot, weight, row: ((row[0] & 1) * half + start, 0, 0)
        elif array.shape[0] == half:
            place = lambda i, *_: (start, 0, 0)
        else:
            place = lambda i, *_: (0, 0, 0)
        return pl.BlockSpec(tuple(pl.Element(n) for n in (count,) + array.shape[1:]), place)

    whole = lambda shape: pl.BlockSpec(shape, lambda i, *_: (0,) * len(shape))
    in_specs = [block(a) for a in operands]
    arrays = [
        pltpu.with_memory_space_constraint(a, pltpu.HBM) if a.shape[0] == images else a
        for a in operands
    ]
    aliases = {}
    numer_shape = (slot_count, band, TILE)
    matched_shape = jax.ShapeDtypeStruct((half, band, side), F32)
    if not first:
        aliases = {3 + len(arrays): 0, 4 + len(arrays): 1}
        arrays += list(carry)
        in_specs += [pl.BlockSpec(memory_space=pl.ANY)] * 2 + [whole(numer_shape)] * 2
    out_shape = [matched_shape] * 2 + [
        jax.ShapeDtypeStruct(numer_shape, F32),
        jax.ShapeDtypeStruct(numer_shape, BF16 if last else F32),
    ]
    out_specs = [block(matched_shape)] * 2 + [whole(numer_shape)] * 2
    scratch = [pltpu.VMEM((side, side), BF16)] * count
    scratch += [pltpu.VMEM((2 * band + 2 * pad, side), BF16)] * count
    scratch += [pltpu.VMEM((2 * band // BLOCK, DEPTH, width), BF16)] * count
    scratch += [pltpu.VMEM((outer * BLOCK, DEPTH), BF16)] * count
    if last:
        scratch.append(pltpu.VMEM(numer_shape, F32))
    return pl.pallas_call(
        functools.partial(match_kernel, start=start, taps=taps, first=first, last=last),
        grid_spec=pltpu.PrefetchScalarGridSpec(
            num_scalar_prefetch=3,
            grid=(1,),
            in_specs=in_specs,
            out_specs=out_specs,
            scratch_shapes=scratch,
        ),
        out_shape=out_shape,
        input_output_aliases=aliases,
        compiler_params=pltpu.CompilerParams(
            vmem_limit_bytes=min(60 * MIB, max(VMEM, 20 * MIB + 16 * slot_count * band * TILE))
        ),
        cost_estimate=pl.CostEstimate(
            flops=count * 2000000000, bytes_accessed=count * 1000000, transcendentals=0
        ),
    )(slots, weights, row, *arrays)


def merge_kernel(own_ref, other_ref, *part_refs):
    each = part_refs[0].shape[0]
    for m, part in enumerate(part_refs):
        boxes = slice(each * m, each * (m + 1))
        part[...] = (own_ref[boxes] + other_ref[boxes].astype(F32)).astype(BF16)


def template_kernel(denom_ref, _, *refs):
    part_refs, template_ref, coadd_ref = refs[:-3], refs[-3], refs[-2]
    for q in range(template_ref.shape[0]):
        total = part_refs[0][q].astype(F32)
        for part in part_refs[1:]:
            total = total + part[q].astype(F32)
        box = (total / jnp.maximum(denom_ref[q], 1.0)).astype(BF16)
        template_ref[q] = box
        coadd_ref[:, TILE * q : TILE * (q + 1)] = box


def difference_kernel(slot_ref, row_ref, own_ref, other_ref, *refs, masks):
    template_refs, out_ref, held = refs[:-2], refs[-2], refs[-1]
    step = pl.program_id(0)
    each = template_refs[0].shape[0]
    count, _, side = own_ref.shape
    tiles = side // TILE

    @pl.when(step == 0)
    def _():
        for m, template in zip(masks, template_refs):
            held[each * m : each * (m + 1)] = template[...]

    def subtract(matched_ref):
        for i in range(count):
            for q in range(tiles):
                slot = slot_ref[(step * count + i) * tiles + q]
                columns = slice(TILE * q, TILE * (q + 1))
                box = held[slot].astype(F32)
                out_ref[i, :, columns] = (matched_ref[i, :, columns] - box).astype(BF16)

    mine = (step * 2 // pl.num_programs(0)) == (row_ref[0] & 1)
    pl.when(mine)(lambda: subtract(own_ref))
    pl.when(jnp.logical_not(mine))(lambda: subtract(other_ref))


def exchange(value, axis, mask):
    size = lax.axis_size(axis)
    return lax.ppermute(value, axis, [(i, i ^ mask) for i in range(size)])


def per_device(
    images,
    warp_rows,
    warp_cols,
    psf_coef,
    taps,
    dest_patch,
    dest_block,
    weight_index,
    weight_table,
    patch_home,
):
    det_count, visit_count, band, side = images.shape
    kernel_count, tap_count = taps.shape
    reach = (tap_count - 1) // 2
    pad = -(-reach // ALIGN) * ALIGN
    span = BLOCK + 2 * pad
    tiles = side // TILE
    det_devices = lax.axis_size("det")
    mine = lax.axis_index("det")
    row = lax.axis_index("row").astype(jnp.int32)
    core = row & 1
    image_count = det_count * visit_count
    half = image_count // 2
    assert lax.axis_size("row") == 4 and image_count == 2 * half
    pixels = images.reshape(image_count, band, side)
    rows = warp_rows.reshape(image_count, band, side)
    cols = warp_cols.reshape(image_count, side, side)
    row_one = row.reshape(1)

    chunks = CHUNKS if sum(CHUNKS) == half else (1,) * half
    starts = [sum(chunks[:c]) for c in range(len(chunks))]
    spans = list(zip(starts, chunks))
    far, cross = [], []

    def send(packed):
        for first, second in zip(packed[::2], packed[1::2]):
            far.append(exchange(first, "row", 2))
            cross.append(exchange(second, "row", 3))

    packed = pack(row_one, pixels, rows, spans[:1], pad, siblings=True)
    sibling_rows = exchange(packed[0], "row", 1)
    sibling = exchange(packed[1], "row", 1)
    send(packed[2:])
    packed = pack(row_one, pixels, rows, spans[1:2], pad, sibling_rows=sibling_rows)
    edge = exchange(packed[-1], "row", 2)
    send(packed[:-1])
    for c in range(2, len(chunks)):
        send(pack(row_one, pixels, rows, spans[c : c + 1], pad, after=[far[c - 2]]))

    with jax.named_scope("profiles"):
        scaled = (psf_coef.reshape(image_count, kernel_count)[:, :, None] * taps).astype(BF16)
        profiles = jnp.einsum(
            "nkt,ku->nut", scaled, taps.astype(BF16), preferred_element_type=F32
        )
        inner = DEPTH // span
        rows_kept = -(-tap_count // inner) * inner
        profiles = jnp.pad(
            profiles,
            (
                (0, 0),
                (0, rows_kept - tap_count + -rows_kept % 8),
                (pad - reach, TILE - tap_count - pad + reach),
            ),
        )
    slots, own_slots, weights, denom = pl.pallas_call(
        functools.partial(target_kernel, tiles=tiles),
        in_specs=[pl.BlockSpec(memory_space=pltpu.SMEM)] * 6
        + [pl.BlockSpec(memory_space=pl.ANY)],
        out_specs=[pl.BlockSpec(memory_space=pltpu.SMEM)] * 4,
        out_shape=[
            jax.ShapeDtypeStruct((image_count * tiles,), jnp.int32),
            jax.ShapeDtypeStruct((half * tiles,), jnp.int32),
            jax.ShapeDtypeStruct((half,), F32),
            jax.ShapeDtypeStruct((tiles,), F32),
        ],
    )(
        jnp.stack([mine.astype(jnp.int32), row]),
        dest_patch.reshape(-1),
        dest_block,
        weight_index.T,
        weight_table,
        patch_home,
        packed[-1],
    )

    carry = None
    slot_count = det_devices * tiles
    for c, (s, n) in enumerate(zip(starts, chunks)):
        operands = (
            pixels, sibling, far[c], cross[c], rows, sibling_rows, edge, cols, profiles,
        )
        carry = match_chunk(
            own_slots, weights, row_one, operands, carry, s, n, tap_count, slot_count,
            c == len(chunks) - 1,
        )
    matched, matched_sent, own_sums, sums_sent = carry
    other_sums = exchange(sums_sent, "row", 1)
    box_shape = (tiles, band, TILE)
    box = jax.ShapeDtypeStruct(box_shape, BF16)
    in_vmem = pl.BlockSpec(memory_space=pltpu.VMEM)
    small = pltpu.CompilerParams(vmem_limit_bytes=4 * MIB + 16 * slot_count * band * TILE)
    parts = pl.pallas_call(
        merge_kernel,
        in_specs=[in_vmem] * 2,
        out_specs=[in_vmem] * det_devices,
        out_shape=[box] * det_devices,
        compiler_params=small,
    )(own_sums, other_sums)
    masks = tuple(range(det_devices - 1, 0, -1)) + (0,)
    received = [exchange(parts[m], "det", m) if m else parts[m] for m in masks]
    anywhere = pl.BlockSpec(memory_space=pl.ANY)
    template, coadd, matched_sent = pl.pallas_call(
        template_kernel,
        in_specs=[pl.BlockSpec(memory_space=pltpu.SMEM), anywhere] + [in_vmem] * det_devices,
        out_specs=[in_vmem] * 2 + [anywhere],
        out_shape=[
            box,
            jax.ShapeDtypeStruct((band, side), BF16),
            jax.ShapeDtypeStruct(matched_sent.shape, F32),
        ],
        input_output_aliases={1: 2},
        compiler_params=small,
    )(denom, matched_sent, *received)
    other_matched = exchange(matched_sent, "row", 1)
    templates = [exchange(template, "det", m) if m else template for m in masks]
    group = 3 if half % 3 == 0 else 1
    steps = half // group

    def half_block(which):
        def place(i, slot, row):
            return (jnp.clip(i - ((row[0] & 1) ^ which) * steps, 0, steps - 1), 0, 0)

        return pl.BlockSpec((group, band, side), place)

    difference = pl.pallas_call(
        functools.partial(difference_kernel, masks=masks),
        grid_spec=pltpu.PrefetchScalarGridSpec(
            num_scalar_prefetch=2,
            grid=(2 * steps,),
            in_specs=[half_block(0), half_block(1)]
            + [pl.BlockSpec(box_shape, lambda i, *_: (0, 0, 0))] * det_devices,
            out_specs=pl.BlockSpec((group, band, side), lambda i, *_: (i, 0, 0)),
            scratch_shapes=[pltpu.VMEM((slot_count, band, TILE), BF16)],
        ),
        out_shape=jax.ShapeDtypeStruct((image_count, band, side), BF16),
        compiler_params=small,
    )(slots, row_one, matched, other_matched, *templates)
    return difference.reshape(images.shape), coadd.reshape(1, band, side)


def solution(mesh):
    placed = (
        P("det", None, "row", None),
        P("det", None, "row", None),
        P("det", None, None, None),
        P("det", None, None),
        P(),
        P(),
        P(),
        P(),
        P(),
        P(),
    )
    return jax.shard_map(
        per_device,
        mesh=mesh,
        in_specs=placed,
        out_specs=(P("det", None, "row", None), P("det", "row", None)),
        check_vma=False,
    )
```

```python
import functools

import jax
import jax.numpy as jnp
from jax import lax
from jax.experimental import pallas as pl
from jax.experimental.pallas import tpu as pltpu
from jax.sharding import PartitionSpec as P

TILE = 128
ALIGN = 16
CHUNKS = (4, 3, 2)
BLOCK = 48
DEPTH = 256
MIB = 1024 * 1024
VMEM = 20 * MIB
F32 = jnp.float32
BF16 = jnp.bfloat16


def pack_kernel(row_ref, *refs, chunks, siblings, edges):
    count = 2 * len(chunks) + siblings + edges
    sems = refs[-1]
    outs, held = refs[-1 - 2 * count : -1 - count], refs[-1 - count : -1]
    pixels_ref, rows_ref = refs[:2]
    half = pixels_ref.shape[0] // 2
    row = row_ref[0]
    core = row & 1
    pieces = []
    kept = list(held)
    if siblings:
        other = pl.ds((1 - core) * half, half)
        pieces += [rows_ref.at[other], pixels_ref.at[other]]
        kept[:1] = [held[0].at[pl.ds(0, half)], held[0].at[pl.ds(half, half)]]
    for s, n in chunks:
        for which in range(2):
            pieces.append(pixels_ref.at[pl.ds((core ^ which) * half + s, n)])
    fetches = [
        pltpu.make_async_copy(piece, place, sems.at[0, i])
        for i, (piece, place) in enumerate(zip(pieces, kept))
    ]
    stores = [
        pltpu.make_async_copy(place, out, sems.at[1, i])
        for i, (place, out) in enumerate(zip(held, outs))
    ]
    if edges:
        pad = outs[-1].shape[1]
        first = jnp.where(row < 2, rows_ref.shape[1] - pad, 0)
        near = pl.ds(pl.multiple_of(first, ALIGN), pad)
        holds = core == (row < 2).astype(jnp.int32)
        own = rows_ref.at[pl.ds(core * half, half), near]
        edge = pltpu.make_async_copy(own, held[-1], sems.at[0, count])
        passed = pltpu.make_async_copy(
            refs[2].at[pl.ds(0, half), near], held[-1], sems.at[0, count]
        )
        pl.when(holds)(edge.start)
        pl.when(jnp.logical_not(holds))(passed.start)
        fetches.append(edge)
    for fetch in fetches[: len(pieces)]:
        fetch.start()
    if siblings:
        fetches.pop(0).wait()
    for fetch, store in zip(fetches, stores):
        fetch.wait()
        store.start()
    for store in stores:
        store.wait()


def pack(row, pixels, rows, chunks, pad, siblings=False, sibling=None, after=()):
    images, band, side = pixels.shape
    half = images // 2
    shapes = [(images, band, side)] if siblings else []
    shapes += [(n, band, side) for _, n in chunks for _ in range(2)]
    arrays = [pltpu.with_memory_space_constraint(a, pltpu.HBM) for a in (pixels, rows)]
    if sibling is not None:
        shapes.append((half, pad, side))
        arrays.append(sibling)
    arrays += after
    anywhere = pl.BlockSpec(memory_space=pl.ANY)
    return pl.pallas_call(
        functools.partial(
            pack_kernel, chunks=chunks, siblings=siblings, edges=sibling is not None
        ),
        in_specs=[pl.BlockSpec(memory_space=pltpu.SMEM)] + [anywhere] * len(arrays),
        out_specs=[anywhere] * len(shapes),
        out_shape=[jax.ShapeDtypeStruct(shape, BF16) for shape in shapes],
        scratch_shapes=[pltpu.VMEM(shape, BF16) for shape in shapes]
        + [pltpu.SemaphoreType.DMA((2, len(shapes) + 1))],
        compiler_params=pltpu.CompilerParams(vmem_limit_bytes=VMEM),
    )(row, *arrays)


def target_kernel(
    place_ref, patch_ref, block_ref, level_ref, table_ref, home_ref, *refs, tiles
):
    large_refs = refs[:4]
    slots_ref, own_ref, weights_ref, denom_ref = refs[5:9]
    kept_refs, sems = refs[9:13], refs[13]
    mine, core = place_ref[0], place_ref[1] & 1
    visits, detectors = level_ref.shape
    pieces = slots_ref.shape[0]
    half = weights_ref.shape[0]
    first = mine * (half * 2)
    copies = [
        pltpu.make_async_copy(large.at[pl.ds(core * half, half)], kept, sems.at[i])
        for i, (large, kept) in enumerate(zip(large_refs, kept_refs))
    ]
    for copy in copies:
        copy.start()

    def slot_of(n):
        return (home_ref[patch_ref[n]] ^ mine) * tiles + block_ref[n]

    def place(i, _):
        slots_ref[i] = slot_of(mine * pieces + i)
        return 0

    def place_own(i, _):
        own_ref[i] = slots_ref[core * half * tiles + i]
        return 0

    def weigh(i, _):
        image = first + core * half + i
        weights_ref[i] = table_ref[level_ref[image % visits, image // visits]]
        return 0

    def add(d, sums):
        for v in range(visits):
            weight = table_ref[level_ref[v, d]]
            for q in range(tiles):
                slot = slot_of((d * visits + v) * tiles + q)
                sums = tuple(
                    total + jnp.where(slot == t, weight, 0.0) for t, total in enumerate(sums)
                )
        return sums

    lax.fori_loop(0, pieces, place, 0)
    lax.fori_loop(0, half * tiles, place_own, 0)
    lax.fori_loop(0, half, weigh, 0)
    sums = lax.fori_loop(0, detectors, add, (jnp.float32(0),) * tiles)
    for t in range(tiles):
        denom_ref[t] = sums[t]
    for copy in copies:
        copy.wait()


def match_kernel(slot_ref, weight_ref, row_ref, *refs, start, count, taps, halves, first, warp, send):
    profile_ref, refs = refs[0], refs[1:]
    if warp:
        pixels_ref, rows_ref, cols_ref, sibling_ref, far_ref, cross_ref, edge_ref = refs[:7]
        refs = refs[7:]
    else:
        warped_ref, refs = refs[0], refs[1:]
    if not first:
        refs = refs[2 * len(halves) :]
    matched_refs = dict(zip(halves, refs))
    refs = refs[len(halves) :]
    numers = dict(zip(halves, refs))
    refs = refs[len(halves) :]
    if send:
        sent_ref, warped_ref, refs = refs[0], refs[1], refs[2:]
    elif warp:
        warped_ref, refs = refs[-1], refs[:-1]
    tables, refs = refs[:count], refs[count:]
    stacks = {m: refs[count * i : count * (i + 1)] for i, m in enumerate(halves)}
    refs = refs[count * len(halves) :]
    _, band, side = matched_refs[halves[0]].shape
    pad = (warped_ref.shape[1] - 2 * band) // 2
    span = BLOCK + 2 * pad
    reach = (taps - 1) // 2
    inner = DEPTH // span
    outer = -(-taps // inner)
    tiles = side // TILE
    width = side + TILE
    blocks = band // BLOCK
    row = row_ref[0]
    core = row & 1

    if first:
        for numer in numers.values():
            numer[...] = jnp.zeros_like(numer)
    if warp:
        for g in range(count):
            image, extended = refs[g], refs[count + g]
            index = start + g
            shards = (pixels_ref.at[index], sibling_ref.at[sibling_ref.shape[0] // 2 + index])
            for mask, shard in enumerate(shards + (far_ref.at[g], cross_ref.at[g])):
                at = pl.multiple_of((row ^ mask) * band, band)
                image[pl.ds(at, band), :] = shard[...]
            edge = edge_ref[index]
            blank = jnp.zeros_like(edge)
            extended[0:pad, :] = jnp.where(row >= 2, edge, blank)
            extended[pad + 2 * band :, :] = jnp.where(row >= 2, blank, edge)
            for which, rows in enumerate((rows_ref, sibling_ref)):
                at = pl.multiple_of(pad + (core ^ which) * band, ALIGN)
                extended[pl.ds(at, band), :] = rows[index]
    for g in range(count):
        profiles = None
        for b in range(inner):
            part = profile_ref[start + g, pl.ds(b, outer, stride=inner), :]
            part = jnp.concatenate([part, jnp.zeros((outer, DEPTH - TILE), F32)], axis=1)
            part = pltpu.roll(part, span * b, 1) if b else part
            profiles = part if profiles is None else profiles + part
        for a in range(outer):
            profile = jnp.broadcast_to(profiles[a : a + 1, :], (BLOCK, DEPTH))
            toeplitz = pltpu.roll(profile, 0, 1, stride=1, stride_axis=0)
            tables[g][BLOCK * a : BLOCK * (a + 1), :] = toeplitz.astype(BF16)
    for g in range(count):
        if warp:
            image, extended = refs[g], refs[count + g]
            by_rows = jnp.dot(extended[...], image[...], preferred_element_type=F32).astype(BF16)
            warped = jnp.dot(by_rows, cols_ref[start + g], preferred_element_type=F32)
            warped_ref[g] = warped.astype(BF16)
        for m in halves:
            at = pl.multiple_of((core ^ m) * band, band)
            ring = warped_ref[g, pl.ds(at, band + 2 * pad), :]
            ring = jnp.concatenate([ring, jnp.zeros((band + 2 * pad, TILE), BF16)], axis=1)
            stack = stacks[m][g]
            stack[:, span * inner :, :] = jnp.zeros((blocks, DEPTH - span * inner, width), BF16)
            for b in range(inner):
                turn = (inner // 2 - b) % width
                shifted = pltpu.roll(ring, turn, 1) if turn else ring
                for k in range(blocks):
                    stack[k, span * b : span * (b + 1), :] = shifted[BLOCK * k : BLOCK * k + span]
    middle = outer // 2
    origin = inner * middle + inner // 2 - reach
    for m in halves:
        for g in range(count):
            index = start + g
            weight = weight_ref[index]
            for k in range(blocks):
                partial = jnp.dot(tables[g][...], stacks[m][g][k], preferred_element_type=F32)
                total = None
                for a in range(outer):
                    turn = (inner * (middle - a) - origin) % width
                    part = partial[BLOCK * a : BLOCK * (a + 1)]
                    part = pltpu.roll(part, turn, 1) if turn else part
                    total = part if total is None else total + part
                matched = total[:, 0:side]
                here = slice(BLOCK * k, BLOCK * (k + 1))
                matched_refs[m][index, here, :] = matched
                for q in range(tiles):
                    slot = slot_ref[index * tiles + q]
                    piece = (weight * matched[:, TILE * q : TILE * (q + 1)]).astype(BF16)
                    numers[m][slot, here, :] += piece.astype(F32)
    if send:
        sent_ref[...] = numers[1][...].astype(BF16)


def match_chunk(scalars, profiles, operands, carry, start, count, taps, slot_count, halves, send=False):
    warp = len(operands) > 1
    if warp:
        half, band, side = operands[0].shape
        tall = 2 * band + 2 * operands[-1].shape[1]
    else:
        _, tall, side = operands[0].shape
        half, band, _ = carry[0].shape
    inner = DEPTH // (BLOCK + tall - 2 * band)
    outer = -(-taps // inner)
    width = side + TILE
    blocks = band // BLOCK
    first = carry is None
    in_vmem = pl.BlockSpec(memory_space=pltpu.VMEM)
    arrays = list(scalars) + [profiles] + list(operands)
    in_specs = [pl.BlockSpec(memory_space=pltpu.SMEM)] * 3 + [in_vmem] * (len(operands) + 1)
    aliases = {}
    if not first:
        aliases = {len(arrays) + i: i for i in range(len(carry))}
        arrays += list(carry)
        in_specs += [in_vmem] * len(carry)
    matched = jax.ShapeDtypeStruct((half, band, side), F32)
    numer_shape = (slot_count, band, TILE)
    out_shape = [matched] * len(halves) + [jax.ShapeDtypeStruct(numer_shape, F32)] * len(halves)
    if send:
        out_shape.append(jax.ShapeDtypeStruct(numer_shape, BF16))
        out_shape.append(jax.ShapeDtypeStruct((count, tall, side), BF16))
    scratch = [pltpu.VMEM((outer * BLOCK, DEPTH), BF16)] * count
    scratch += [pltpu.VMEM((blocks, DEPTH, width), BF16)] * (count * len(halves))
    if warp:
        scratch += [pltpu.VMEM((side, side), BF16)] * count
        scratch += [pltpu.VMEM((tall, side), BF16)] * count
        if not send:
            scratch.append(pltpu.VMEM((count, tall, side), BF16))
    return pl.pallas_call(
        functools.partial(
            match_kernel,
            start=start,
            count=count,
            taps=taps,
            halves=halves,
            first=first,
            warp=warp,
            send=send,
        ),
        in_specs=in_specs,
        out_specs=[in_vmem] * len(out_shape),
        scratch_shapes=scratch,
        out_shape=out_shape,
        input_output_aliases=aliases,
        compiler_params=pltpu.CompilerParams(vmem_limit_bytes=VMEM),
        cost_estimate=pl.CostEstimate(
            flops=count * 1000000000 * len(halves), bytes_accessed=count * 1000000, transcendentals=0
        ),
    )(*arrays)


def merge_kernel(own_ref, other_ref, *part_refs):
    each = part_refs[0].shape[0]
    for m, part in enumerate(part_refs):
        boxes = slice(each * m, each * (m + 1))
        part[...] = (own_ref[boxes] + other_ref[boxes].astype(F32)).astype(BF16)


def template_kernel(denom_ref, _, *refs):
    part_refs, template_ref, coadd_ref = refs[:-3], refs[-3], refs[-2]
    for q in range(template_ref.shape[0]):
        total = part_refs[0][q].astype(F32)
        for part in part_refs[1:]:
            total = total + part[q].astype(F32)
        box = (total / jnp.maximum(denom_ref[q], 1.0)).astype(BF16)
        template_ref[q] = box
        coadd_ref[:, TILE * q : TILE * (q + 1)] = box


def difference_kernel(slot_ref, row_ref, own_ref, other_ref, *refs, masks):
    template_refs, out_ref, held = refs[:-2], refs[-2], refs[-1]
    step = pl.program_id(0)
    each = template_refs[0].shape[0]
    count, _, side = own_ref.shape
    tiles = side // TILE

    @pl.when(step == 0)
    def _():
        for m, template in zip(masks, template_refs):
            held[each * m : each * (m + 1)] = template[...]

    def subtract(matched_ref):
        for i in range(count):
            for q in range(tiles):
                slot = slot_ref[(step * count + i) * tiles + q]
                columns = slice(TILE * q, TILE * (q + 1))
                box = held[slot].astype(F32)
                out_ref[i, :, columns] = (matched_ref[i, :, columns] - box).astype(BF16)

    mine = (step * 2 // pl.num_programs(0)) == (row_ref[0] & 1)
    pl.when(mine)(lambda: subtract(own_ref))
    pl.when(jnp.logical_not(mine))(lambda: subtract(other_ref))


def exchange(value, axis, mask):
    size = lax.axis_size(axis)
    return lax.ppermute(value, axis, [(i, i ^ mask) for i in range(size)])


def per_device(
    images,
    warp_rows,
    warp_cols,
    psf_coef,
    taps,
    dest_patch,
    dest_block,
    weight_index,
    weight_table,
    patch_home,
):
    det_count, visit_count, band, side = images.shape
    kernel_count, tap_count = taps.shape
    reach = (tap_count - 1) // 2
    pad = -(-reach // ALIGN) * ALIGN
    span = BLOCK + 2 * pad
    tiles = side // TILE
    det_devices = lax.axis_size("det")
    mine = lax.axis_index("det")
    row = lax.axis_index("row").astype(jnp.int32)
    core = row & 1
    image_count = det_count * visit_count
    half = image_count // 2
    assert lax.axis_size("row") == 4 and image_count == 2 * half
    pixels = images.reshape(image_count, band, side)
    rows = warp_rows.reshape(image_count, band, side)
    cols = warp_cols.reshape(image_count, side, side)
    row_one = row.reshape(1)

    chunks = CHUNKS if sum(CHUNKS) == half else (1,) * half
    starts = [sum(chunks[:c]) for c in range(len(chunks))]
    spans = list(zip(starts, chunks))
    far, cross = [], []

    def send(packed):
        for first, second in zip(packed[::2], packed[1::2]):
            far.append(exchange(first, "row", 2))
            cross.append(exchange(second, "row", 3))

    packed = pack(row_one, pixels, rows, spans[:1], pad, siblings=True)
    sibling = exchange(packed[0], "row", 1)
    send(packed[1:])
    packed = pack(row_one, pixels, rows, spans[2:], pad, sibling=sibling)
    edge = exchange(packed[-1], "row", 2)
    send(pack(row_one, pixels, rows, spans[1:2], pad, after=[far[0]]))
    send(packed[:-1])

    with jax.named_scope("profiles"):
        scaled = (psf_coef.reshape(image_count, kernel_count)[:, :, None] * taps).astype(BF16)
        profiles = jnp.einsum(
            "nkt,ku->nut", scaled, taps.astype(BF16), preferred_element_type=F32
        )
        inner = DEPTH // span
        rows_kept = -(-tap_count // inner) * inner
        profiles = jnp.pad(
            profiles,
            (
                (0, 0),
                (0, rows_kept - tap_count + -rows_kept % 8),
                (pad - reach, TILE - tap_count - pad + reach),
            ),
        )
    anywhere = pl.BlockSpec(memory_space=pl.ANY)
    in_vmem = pl.BlockSpec(memory_space=pltpu.VMEM)
    large = (pixels, rows, cols, profiles)
    slots, own_slots, weights, denom, *kept = pl.pallas_call(
        functools.partial(target_kernel, tiles=tiles),
        in_specs=[pl.BlockSpec(memory_space=pltpu.SMEM)] * 6 + [anywhere] * 5,
        out_specs=[pl.BlockSpec(memory_space=pltpu.SMEM)] * 4 + [in_vmem] * 4,
        out_shape=[
            jax.ShapeDtypeStruct((image_count * tiles,), jnp.int32),
            jax.ShapeDtypeStruct((half * tiles,), jnp.int32),
            jax.ShapeDtypeStruct((half,), F32),
            jax.ShapeDtypeStruct((tiles,), F32),
        ]
        + [jax.ShapeDtypeStruct((half,) + a.shape[1:], a.dtype) for a in large],
        scratch_shapes=[pltpu.SemaphoreType.DMA((len(large),))],
        compiler_params=pltpu.CompilerParams(vmem_limit_bytes=VMEM),
    )(
        jnp.stack([mine.astype(jnp.int32), row]),
        dest_patch.reshape(-1),
        dest_block,
        weight_index.T,
        weight_table,
        patch_home,
        *[pltpu.with_memory_space_constraint(a, pltpu.HBM) for a in large],
        packed[-1],
    )

    carry = None
    slot_count = det_devices * tiles
    scalars = (own_slots, weights, row_one)
    common = (tap_count, slot_count)
    for c, (s, n) in enumerate(spans):
        operands = tuple(kept[:3]) + (sibling, far[c], cross[c], edge)
        if c < len(spans) - 1:
            carry = match_chunk(scalars, kept[3], operands, carry, s, n, *common, (0, 1))
    matched_sent, _, sums_sent, warped = match_chunk(
        scalars, kept[3], operands, carry[1::2], s, n, *common, (1,), send=True
    )
    other_sums = exchange(sums_sent, "row", 1)
    matched, own_sums = match_chunk(
        scalars, kept[3], (warped,), carry[0::2], s, n, *common, (0,)
    )
    box_shape = (tiles, band, TILE)
    box = jax.ShapeDtypeStruct(box_shape, BF16)
    small = pltpu.CompilerParams(vmem_limit_bytes=4 * MIB + 16 * slot_count * band * TILE)
    parts = pl.pallas_call(
        merge_kernel,
        in_specs=[in_vmem] * 2,
        out_specs=[in_vmem] * det_devices,
        out_shape=[box] * det_devices,
        compiler_params=small,
    )(own_sums, other_sums)
    masks = tuple(range(det_devices - 1, 0, -1)) + (0,)
    received = [exchange(parts[m], "det", m) if m else parts[m] for m in masks]
    template, coadd, matched_sent = pl.pallas_call(
        template_kernel,
        in_specs=[pl.BlockSpec(memory_space=pltpu.SMEM), anywhere] + [in_vmem] * det_devices,
        out_specs=[in_vmem] * 2 + [anywhere],
        out_shape=[
            box,
            jax.ShapeDtypeStruct((band, side), BF16),
            jax.ShapeDtypeStruct(matched_sent.shape, F32),
        ],
        input_output_aliases={1: 2},
        compiler_params=small,
    )(denom, matched_sent, *received)
    other_matched = exchange(matched_sent, "row", 1)
    evens = tuple(range(det_devices - 2, 0, -2))
    passed = {0: template}
    for m in evens:
        passed[m] = exchange(template, "det", m)
    for m in evens + (0,):
        passed[m ^ 1] = exchange(passed[m], "det", 1)
    templates = [passed[m] for m in masks]
    group = 3 if half % 3 == 0 else 1
    steps = half // group

    def half_block(which):
        def place(i, slot, row):
            return (jnp.clip(i - ((row[0] & 1) ^ which) * steps, 0, steps - 1), 0, 0)

        return pl.BlockSpec((group, band, side), place)

    difference = pl.pallas_call(
        functools.partial(difference_kernel, masks=masks),
        grid_spec=pltpu.PrefetchScalarGridSpec(
            num_scalar_prefetch=2,
            grid=(2 * steps,),
            in_specs=[half_block(0), half_block(1)]
            + [pl.BlockSpec(box_shape, lambda i, *_: (0, 0, 0))] * det_devices,
            out_specs=pl.BlockSpec((group, band, side), lambda i, *_: (i, 0, 0)),
            scratch_shapes=[pltpu.VMEM((slot_count, band, TILE), BF16)],
        ),
        out_shape=jax.ShapeDtypeStruct((image_count, band, side), BF16),
        compiler_params=small,
    )(slots, row_one, matched, other_matched, *templates)
    return difference.reshape(images.shape), coadd.reshape(1, band, side)


def solution(mesh):
    placed = (
        P("det", None, "row", None),
        P("det", None, "row", None),
        P("det", None, None, None),
        P("det", None, None),
        P(),
        P(),
        P(),
        P(),
        P(),
        P(),
    )
    return jax.shard_map(
        per_device,
        mesh=mesh,
        in_specs=placed,
        out_specs=(P("det", None, "row", None), P("det", "row", None)),
        check_vma=False,
    )
```

```python
import functools

import jax
import jax.numpy as jnp
from jax import lax
from jax.experimental import pallas as pl
from jax.experimental.pallas import tpu as pltpu
from jax.sharding import PartitionSpec as P

TILE = 128
ALIGN = 16
CHUNKS = (4, 3, 2)
BLOCK = 48
DEPTH = 256
MIB = 1024 * 1024
VMEM = 20 * MIB
F32 = jnp.float32
BF16 = jnp.bfloat16


def pack_kernel(row_ref, *refs, chunks, siblings, edges):
    count = 2 * len(chunks) + siblings + edges
    sems = refs[-1]
    outs, held = refs[-1 - 2 * count : -1 - count], refs[-1 - count : -1]
    pixels_ref, rows_ref = refs[:2]
    half = pixels_ref.shape[0] // 2
    row = row_ref[0]
    core = row & 1
    pieces = []
    kept = list(held)
    if siblings:
        other = pl.ds((1 - core) * half, half)
        pieces += [rows_ref.at[other], pixels_ref.at[other]]
        kept[:1] = [held[0].at[pl.ds(0, half)], held[0].at[pl.ds(half, half)]]
    for s, n in chunks:
        for which in range(2):
            pieces.append(pixels_ref.at[pl.ds((core ^ which) * half + s, n)])
    fetches = [
        pltpu.make_async_copy(piece, place, sems.at[0, i])
        for i, (piece, place) in enumerate(zip(pieces, kept))
    ]
    stores = [
        pltpu.make_async_copy(place, out, sems.at[1, i])
        for i, (place, out) in enumerate(zip(held, outs))
    ]
    if edges:
        pad = outs[-1].shape[1]
        first = jnp.where(row < 2, rows_ref.shape[1] - pad, 0)
        near = pl.ds(pl.multiple_of(first, ALIGN), pad)
        holds = core == (row < 2).astype(jnp.int32)
        own = rows_ref.at[pl.ds(core * half, half), near]
        edge = pltpu.make_async_copy(own, held[-1], sems.at[0, count])
        passed = pltpu.make_async_copy(
            refs[2].at[pl.ds(0, half), near], held[-1], sems.at[0, count]
        )
        pl.when(holds)(edge.start)
        pl.when(jnp.logical_not(holds))(passed.start)
        fetches.append(edge)
    for fetch in fetches[: len(pieces)]:
        fetch.start()
    if siblings:
        fetches.pop(0).wait()
    for fetch, store in zip(fetches, stores):
        fetch.wait()
        store.start()
    for store in stores:
        store.wait()


def pack(row, pixels, rows, chunks, pad, siblings=False, sibling=None, after=()):
    images, band, side = pixels.shape
    half = images // 2
    shapes = [(images, band, side)] if siblings else []
    shapes += [(n, band, side) for _, n in chunks for _ in range(2)]
    arrays = [pltpu.with_memory_space_constraint(a, pltpu.HBM) for a in (pixels, rows)]
    if sibling is not None:
        shapes.append((half, pad, side))
        arrays.append(sibling)
    arrays += after
    anywhere = pl.BlockSpec(memory_space=pl.ANY)
    return pl.pallas_call(
        functools.partial(
            pack_kernel, chunks=chunks, siblings=siblings, edges=sibling is not None
        ),
        in_specs=[pl.BlockSpec(memory_space=pltpu.SMEM)] + [anywhere] * len(arrays),
        out_specs=[anywhere] * len(shapes),
        out_shape=[jax.ShapeDtypeStruct(shape, BF16) for shape in shapes],
        scratch_shapes=[pltpu.VMEM(shape, BF16) for shape in shapes]
        + [pltpu.SemaphoreType.DMA((2, len(shapes) + 1))],
        compiler_params=pltpu.CompilerParams(vmem_limit_bytes=VMEM),
    )(row, *arrays)


def target_kernel(
    place_ref, patch_ref, block_ref, level_ref, table_ref, home_ref, *refs, tiles
):
    large_refs = refs[:4]
    slots_ref, own_ref, weights_ref, denom_ref = refs[5:9]
    kept_refs, sems = refs[9:13], refs[13]
    mine, core = place_ref[0], place_ref[1] & 1
    visits, detectors = level_ref.shape
    pieces = slots_ref.shape[0]
    half = weights_ref.shape[0]
    first = mine * (half * 2)
    copies = [
        pltpu.make_async_copy(large.at[pl.ds(core * half, half)], kept, sems.at[i])
        for i, (large, kept) in enumerate(zip(large_refs, kept_refs))
    ]
    for copy in copies:
        copy.start()

    def slot_of(n):
        return (home_ref[patch_ref[n]] ^ mine) * tiles + block_ref[n]

    def place(i, _):
        slots_ref[i] = slot_of(mine * pieces + i)
        return 0

    def place_own(i, _):
        own_ref[i] = slots_ref[core * half * tiles + i]
        return 0

    def weigh(i, _):
        image = first + core * half + i
        weights_ref[i] = table_ref[level_ref[image % visits, image // visits]]
        return 0

    def add(d, sums):
        for v in range(visits):
            weight = table_ref[level_ref[v, d]]
            for q in range(tiles):
                slot = slot_of((d * visits + v) * tiles + q)
                sums = tuple(
                    total + jnp.where(slot == t, weight, 0.0) for t, total in enumerate(sums)
                )
        return sums

    lax.fori_loop(0, pieces, place, 0)
    lax.fori_loop(0, half * tiles, place_own, 0)
    lax.fori_loop(0, half, weigh, 0)
    sums = lax.fori_loop(0, detectors, add, (jnp.float32(0),) * tiles)
    for t in range(tiles):
        denom_ref[t] = sums[t]
    for copy in copies:
        copy.wait()


def match_kernel(slot_ref, weight_ref, row_ref, *refs, start, count, taps, halves, first, warp, send):
    profile_ref, refs = refs[0], refs[1:]
    if warp:
        pixels_ref, rows_ref, cols_ref, sibling_ref, far_ref, cross_ref, edge_ref = refs[:7]
        refs = refs[7:]
    else:
        warped_ref, refs = refs[0], refs[1:]
    if not first:
        refs = refs[2 * len(halves) :]
    matched_refs = dict(zip(halves, refs))
    refs = refs[len(halves) :]
    numers = dict(zip(halves, refs))
    refs = refs[len(halves) :]
    if send:
        sent_ref, warped_ref, refs = refs[0], refs[1], refs[2:]
    elif warp:
        warped_ref, refs = refs[-1], refs[:-1]
    tables, refs = refs[:count], refs[count:]
    stacks = {m: refs[count * i : count * (i + 1)] for i, m in enumerate(halves)}
    refs = refs[count * len(halves) :]
    _, band, side = matched_refs[halves[0]].shape
    pad = (warped_ref.shape[1] - 2 * band) // 2
    span = BLOCK + 2 * pad
    reach = (taps - 1) // 2
    inner = DEPTH // span
    outer = -(-taps // inner)
    tiles = side // TILE
    width = side + TILE
    blocks = band // BLOCK
    row = row_ref[0]
    core = row & 1

    if first:
        for numer in numers.values():
            numer[...] = jnp.zeros_like(numer)
    if warp:
        for g in range(count):
            image, extended = refs[g], refs[count + g]
            index = start + g
            shards = (pixels_ref.at[index], sibling_ref.at[sibling_ref.shape[0] // 2 + index])
            for mask, shard in enumerate(shards + (far_ref.at[g], cross_ref.at[g])):
                at = pl.multiple_of((row ^ mask) * band, band)
                image[pl.ds(at, band), :] = shard[...]
            edge = edge_ref[index]
            blank = jnp.zeros_like(edge)
            extended[0:pad, :] = jnp.where(row >= 2, edge, blank)
            extended[pad + 2 * band :, :] = jnp.where(row >= 2, blank, edge)
            for which, rows in enumerate((rows_ref, sibling_ref)):
                at = pl.multiple_of(pad + (core ^ which) * band, ALIGN)
                extended[pl.ds(at, band), :] = rows[index]
    for g in range(count):
        profiles = None
        for b in range(inner):
            part = profile_ref[start + g, pl.ds(b, outer, stride=inner), :]
            part = jnp.concatenate([part, jnp.zeros((outer, DEPTH - TILE), F32)], axis=1)
            part = pltpu.roll(part, span * b, 1) if b else part
            profiles = part if profiles is None else profiles + part
        for a in range(outer):
            profile = jnp.broadcast_to(profiles[a : a + 1, :], (BLOCK, DEPTH))
            toeplitz = pltpu.roll(profile, 0, 1, stride=1, stride_axis=0)
            tables[g][BLOCK * a : BLOCK * (a + 1), :] = toeplitz.astype(BF16)
    for g in range(count):
        if warp:
            image, extended = refs[g], refs[count + g]
            by_rows = jnp.dot(extended[...], image[...], preferred_element_type=F32).astype(BF16)
            warped = jnp.dot(by_rows, cols_ref[start + g], preferred_element_type=F32)
            warped_ref[g] = warped.astype(BF16)
        for m in halves:
            at = pl.multiple_of((core ^ m) * band, band)
            ring = warped_ref[g, pl.ds(at, band + 2 * pad), :]
            ring = jnp.concatenate([ring, jnp.zeros((band + 2 * pad, TILE), BF16)], axis=1)
            stack = stacks[m][g]
            stack[:, span * inner :, :] = jnp.zeros((blocks, DEPTH - span * inner, width), BF16)
            for b in range(inner):
                turn = (inner // 2 - b) % width
                shifted = pltpu.roll(ring, turn, 1) if turn else ring
                for k in range(blocks):
                    stack[k, span * b : span * (b + 1), :] = shifted[BLOCK * k : BLOCK * k + span]
    middle = outer // 2
    origin = inner * middle + inner // 2 - reach
    for m in halves:
        for g in range(count):
            index = start + g
            weight = weight_ref[index]
            for k in range(blocks):
                partial = jnp.dot(tables[g][...], stacks[m][g][k], preferred_element_type=F32)
                total = None
                for a in range(outer):
                    turn = (inner * (middle - a) - origin) % width
                    part = partial[BLOCK * a : BLOCK * (a + 1)]
                    part = pltpu.roll(part, turn, 1) if turn else part
                    total = part if total is None else total + part
                matched = total[:, 0:side]
                here = slice(BLOCK * k, BLOCK * (k + 1))
                matched_refs[m][index, here, :] = matched
                for q in range(tiles):
                    slot = slot_ref[index * tiles + q]
                    piece = (weight * matched[:, TILE * q : TILE * (q + 1)]).astype(BF16)
                    numers[m][slot, here, :] += piece.astype(F32)
    if send:
        sent_ref[...] = numers[1][...].astype(BF16)


def match_chunk(scalars, profiles, operands, carry, start, count, taps, slot_count, halves, send=False):
    warp = len(operands) > 1
    if warp:
        half, band, side = operands[0].shape
        tall = 2 * band + 2 * operands[-1].shape[1]
    else:
        _, tall, side = operands[0].shape
        half, band, _ = carry[0].shape
    inner = DEPTH // (BLOCK + tall - 2 * band)
    outer = -(-taps // inner)
    width = side + TILE
    blocks = band // BLOCK
    first = carry is None
    in_vmem = pl.BlockSpec(memory_space=pltpu.VMEM)
    arrays = list(scalars) + [profiles] + list(operands)
    in_specs = [pl.BlockSpec(memory_space=pltpu.SMEM)] * 3 + [in_vmem] * (len(operands) + 1)
    aliases = {}
    if not first:
        aliases = {len(arrays) + i: i for i in range(len(carry))}
        arrays += list(carry)
        in_specs += [in_vmem] * len(carry)
    matched = jax.ShapeDtypeStruct((half, band, side), F32)
    numer_shape = (slot_count, band, TILE)
    out_shape = [matched] * len(halves) + [jax.ShapeDtypeStruct(numer_shape, F32)] * len(halves)
    if send:
        out_shape.append(jax.ShapeDtypeStruct(numer_shape, BF16))
        out_shape.append(jax.ShapeDtypeStruct((count, tall, side), BF16))
    scratch = [pltpu.VMEM((outer * BLOCK, DEPTH), BF16)] * count
    scratch += [pltpu.VMEM((blocks, DEPTH, width), BF16)] * (count * len(halves))
    if warp:
        scratch += [pltpu.VMEM((side, side), BF16)] * count
        scratch += [pltpu.VMEM((tall, side), BF16)] * count
        if not send:
            scratch.append(pltpu.VMEM((count, tall, side), BF16))
    return pl.pallas_call(
        functools.partial(
            match_kernel,
            start=start,
            count=count,
            taps=taps,
            halves=halves,
            first=first,
            warp=warp,
            send=send,
        ),
        in_specs=in_specs,
        out_specs=[in_vmem] * len(out_shape),
        scratch_shapes=scratch,
        out_shape=out_shape,
        input_output_aliases=aliases,
        compiler_params=pltpu.CompilerParams(vmem_limit_bytes=VMEM),
        cost_estimate=pl.CostEstimate(
            flops=count * 1000000000 * len(halves), bytes_accessed=count * 1000000, transcendentals=0
        ),
    )(*arrays)


def merge_kernel(own_ref, other_ref, *part_refs):
    each = part_refs[0].shape[0]
    for m, part in enumerate(part_refs):
        boxes = slice(each * m, each * (m + 1))
        part[...] = (own_ref[boxes] + other_ref[boxes].astype(F32)).astype(part.dtype)


def add_kernel(own_ref, other_ref, total_ref):
    total_ref[...] = (own_ref[...] + other_ref[...].astype(F32)).astype(BF16)


def template_kernel(denom_ref, _, *refs):
    part_refs, template_ref, coadd_ref = refs[:-3], refs[-3], refs[-2]
    for q in range(template_ref.shape[0]):
        total = part_refs[0][q].astype(F32)
        for part in part_refs[1:]:
            total = total + part[q].astype(F32)
        box = (total / jnp.maximum(denom_ref[q], 1.0)).astype(BF16)
        template_ref[q] = box
        coadd_ref[:, TILE * q : TILE * (q + 1)] = box


def difference_kernel(slot_ref, row_ref, own_ref, other_ref, *refs, group):
    template_refs, out_ref = refs[:-4], refs[-4]
    held, ready, sems = refs[-3:]
    each = template_refs[0].shape[0]
    half, _, side = own_ref.shape
    tiles = side // TILE
    core = row_ref[0] & 1
    for m, template in enumerate(template_refs):
        held[each * m : each * (m + 1)] = template[...]
    copies = []
    for which, matched_ref in enumerate((own_ref, other_ref)):
        for first in range(0, half, group):
            at = (core ^ which) * half + first
            for i in range(group):
                for q in range(tiles):
                    slot = slot_ref[(at + i) * tiles + q]
                    columns = slice(TILE * q, TILE * (q + 1))
                    box = held[slot].astype(F32)
                    value = (matched_ref[first + i, :, columns] - box).astype(BF16)
                    ready[which * half + first + i, :, columns] = value
            copies.append(
                pltpu.make_async_copy(
                    ready.at[pl.ds(which * half + first, group)],
                    out_ref.at[pl.ds(at, group)],
                    sems.at[len(copies)],
                )
            )
            copies[-1].start()
    for copy in copies:
        copy.wait()


def exchange(value, axis, mask):
    size = lax.axis_size(axis)
    return lax.ppermute(value, axis, [(i, i ^ mask) for i in range(size)])


def per_device(
    images,
    warp_rows,
    warp_cols,
    psf_coef,
    taps,
    dest_patch,
    dest_block,
    weight_index,
    weight_table,
    patch_home,
):
    det_count, visit_count, band, side = images.shape
    kernel_count, tap_count = taps.shape
    reach = (tap_count - 1) // 2
    pad = -(-reach // ALIGN) * ALIGN
    span = BLOCK + 2 * pad
    tiles = side // TILE
    det_devices = lax.axis_size("det")
    mine = lax.axis_index("det")
    row = lax.axis_index("row").astype(jnp.int32)
    core = row & 1
    image_count = det_count * visit_count
    half = image_count // 2
    assert lax.axis_size("row") == 4 and image_count == 2 * half
    pixels = images.reshape(image_count, band, side)
    rows = warp_rows.reshape(image_count, band, side)
    cols = warp_cols.reshape(image_count, side, side)
    row_one = row.reshape(1)

    chunks = CHUNKS if sum(CHUNKS) == half else (1,) * half
    starts = [sum(chunks[:c]) for c in range(len(chunks))]
    spans = list(zip(starts, chunks))
    far, cross = [], []

    def send(packed):
        for first, second in zip(packed[::2], packed[1::2]):
            far.append(exchange(first, "row", 2))
            cross.append(exchange(second, "row", 3))

    packed = pack(row_one, pixels, rows, spans[:1], pad, siblings=True)
    sibling = exchange(packed[0], "row", 1)
    send(packed[1:])
    packed = pack(row_one, pixels, rows, spans[2:], pad, sibling=sibling)
    edge = exchange(packed[-1], "row", 2)
    send(pack(row_one, pixels, rows, spans[1:2], pad, after=[far[0]]))
    send(packed[:-1])

    with jax.named_scope("profiles"):
        scaled = (psf_coef.reshape(image_count, kernel_count)[:, :, None] * taps).astype(BF16)
        profiles = jnp.einsum(
            "nkt,ku->nut", scaled, taps.astype(BF16), preferred_element_type=F32
        )
        inner = DEPTH // span
        rows_kept = -(-tap_count // inner) * inner
        profiles = jnp.pad(
            profiles,
            (
                (0, 0),
                (0, rows_kept - tap_count + -rows_kept % 8),
                (pad - reach, TILE - tap_count - pad + reach),
            ),
        )
    anywhere = pl.BlockSpec(memory_space=pl.ANY)
    in_vmem = pl.BlockSpec(memory_space=pltpu.VMEM)
    large = (pixels, rows, cols, profiles)
    slots, own_slots, weights, denom, *kept = pl.pallas_call(
        functools.partial(target_kernel, tiles=tiles),
        in_specs=[pl.BlockSpec(memory_space=pltpu.SMEM)] * 6 + [anywhere] * 5,
        out_specs=[pl.BlockSpec(memory_space=pltpu.SMEM)] * 4 + [in_vmem] * 4,
        out_shape=[
            jax.ShapeDtypeStruct((image_count * tiles,), jnp.int32),
            jax.ShapeDtypeStruct((half * tiles,), jnp.int32),
            jax.ShapeDtypeStruct((half,), F32),
            jax.ShapeDtypeStruct((tiles,), F32),
        ]
        + [jax.ShapeDtypeStruct((half,) + a.shape[1:], a.dtype) for a in large],
        scratch_shapes=[pltpu.SemaphoreType.DMA((len(large),))],
        compiler_params=pltpu.CompilerParams(vmem_limit_bytes=VMEM),
    )(
        jnp.stack([mine.astype(jnp.int32), row]),
        dest_patch.reshape(-1),
        dest_block,
        weight_index.T,
        weight_table,
        patch_home,
        *[pltpu.with_memory_space_constraint(a, pltpu.HBM) for a in large],
        packed[-1],
    )

    carry = None
    slot_count = det_devices * tiles
    scalars = (own_slots, weights, row_one)
    common = (tap_count, slot_count)
    for c, (s, n) in enumerate(spans):
        operands = tuple(kept[:3]) + (sibling, far[c], cross[c], edge)
        if c < len(spans) - 1:
            carry = match_chunk(scalars, kept[3], operands, carry, s, n, *common, (0, 1))
    matched_sent, _, sums_sent, warped = match_chunk(
        scalars, kept[3], operands, carry[1::2], s, n, *common, (1,), send=True
    )
    other_sums = exchange(sums_sent, "row", 1)
    matched, own_sums = match_chunk(
        scalars, kept[3], (warped,), carry[0::2], s, n, *common, (0,)
    )
    box_shape = (tiles, band, TILE)
    box = jax.ShapeDtypeStruct(box_shape, BF16)
    small = pltpu.CompilerParams(vmem_limit_bytes=4 * MIB + 16 * slot_count * band * TILE)
    parts = pl.pallas_call(
        merge_kernel,
        in_specs=[in_vmem] * 2,
        out_specs=[in_vmem] * det_devices,
        out_shape=[
            jax.ShapeDtypeStruct(box_shape, BF16 if m % 2 else F32) for m in range(det_devices)
        ],
        compiler_params=small,
    )(own_sums, other_sums)
    evens = tuple(range(det_devices - 2, 0, -2))
    across = {m: exchange(parts[m ^ 1], "det", 1) for m in evens + (0,)}
    received = [parts[0], across[0]]
    for m in evens:
        total = pl.pallas_call(
            add_kernel,
            in_specs=[in_vmem] * 2,
            out_specs=in_vmem,
            out_shape=box,
            compiler_params=small,
        )(parts[m], across[m])
        received.append(exchange(total, "det", m))
    template, coadd, matched_sent = pl.pallas_call(
        template_kernel,
        in_specs=[pl.BlockSpec(memory_space=pltpu.SMEM), anywhere] + [in_vmem] * len(received),
        out_specs=[in_vmem] * 2 + [anywhere],
        out_shape=[
            box,
            jax.ShapeDtypeStruct((band, side), BF16),
            jax.ShapeDtypeStruct(matched_sent.shape, F32),
        ],
        input_output_aliases={1: 2},
        compiler_params=small,
    )(denom, matched_sent, *received)
    other_matched = exchange(matched_sent, "row", 1)
    passed = {0: template}
    for m in evens:
        passed[m] = exchange(template, "det", m)
    for m in evens + (0,):
        passed[m ^ 1] = exchange(passed[m], "det", 1)
    templates = [passed[m] for m in range(det_devices)]
    group = 3 if half % 3 == 0 else 1
    difference = pl.pallas_call(
        functools.partial(difference_kernel, group=group),
        in_specs=[pl.BlockSpec(memory_space=pltpu.SMEM)] * 2 + [in_vmem] * (2 + det_devices),
        out_specs=anywhere,
        scratch_shapes=[
            pltpu.VMEM((slot_count, band, TILE), BF16),
            pltpu.VMEM((image_count, band, side), BF16),
            pltpu.SemaphoreType.DMA((image_count // group,)),
        ],
        out_shape=jax.ShapeDtypeStruct((image_count, band, side), BF16),
        compiler_params=small,
    )(slots, row_one, matched, other_matched, *templates)
    return difference.reshape(images.shape), coadd.reshape(1, band, side)


def solution(mesh):
    placed = (
        P("det", None, "row", None),
        P("det", None, "row", None),
        P("det", None, None, None),
        P("det", None, None),
        P(),
        P(),
        P(),
        P(),
        P(),
        P(),
    )
    return jax.shard_map(
        per_device,
        mesh=mesh,
        in_specs=placed,
        out_specs=(P("det", None, "row", None), P("det", "row", None)),
        check_vma=False,
    )
```

```python
import functools

import jax
import jax.numpy as jnp
from jax import lax
from jax.experimental import pallas as pl
from jax.experimental.pallas import tpu as pltpu
from jax.sharding import PartitionSpec as P

TILE = 128
ALIGN = 16
CHUNKS = (4, 3, 2)
BLOCK = 48
DEPTH = 256
MIB = 1024 * 1024
VMEM = 20 * MIB
F32 = jnp.float32
BF16 = jnp.bfloat16


def pack_kernel(row_ref, *refs, chunks, edges):
    sems = refs[-1]
    outs = list(refs[-1 - 2 * len(chunks) - edges : -1])
    pixels_ref, rows_ref = refs[:2]
    half = pixels_ref.shape[0] // 2
    row = row_ref[0]
    core = row & 1
    pieces = []
    for s, n in chunks:
        for which in range(2):
            pieces.append(pixels_ref.at[pl.ds((core ^ which) * half + s, n)])
    copies = [
        pltpu.make_async_copy(piece, out, sems.at[i]) for i, (piece, out) in enumerate(zip(pieces, outs))
    ]
    for copy in copies:
        copy.start()
    if edges:
        pad = outs[-1].shape[1]
        first = jnp.where(row < 2, rows_ref.shape[1] - pad, 0)
        near = pl.ds(pl.multiple_of(first, ALIGN), pad)
        holds = core == (row < 2).astype(jnp.int32)
        own = rows_ref.at[pl.ds(core * half, half), near]
        edge = pltpu.make_async_copy(own, outs[-1], sems.at[len(pieces)])
        passed = pltpu.make_async_copy(
            refs[2].at[pl.ds(core * half, half), near], outs[-1], sems.at[len(pieces)]
        )
        pl.when(holds)(edge.start)
        pl.when(jnp.logical_not(holds))(passed.start)
        copies.append(edge)
    for copy in copies:
        copy.wait()


def pack(row, pixels, rows, chunks, pad, sibling_rows=None, after=()):
    images, band, side = pixels.shape
    half = images // 2
    shapes = [(n, band, side) for _, n in chunks for _ in range(2)]
    arrays = [pltpu.with_memory_space_constraint(a, pltpu.HBM) for a in (pixels, rows)]
    if sibling_rows is not None:
        shapes.append((half, pad, side))
        arrays.append(sibling_rows)
    arrays += after
    anywhere = pl.BlockSpec(memory_space=pl.ANY)
    return pl.pallas_call(
        functools.partial(
            pack_kernel, chunks=chunks, edges=sibling_rows is not None
        ),
        in_specs=[pl.BlockSpec(memory_space=pltpu.SMEM)] + [anywhere] * len(arrays),
        out_specs=[pl.BlockSpec(memory_space=pltpu.VMEM)] * len(shapes),
        out_shape=[jax.ShapeDtypeStruct(shape, BF16) for shape in shapes],
        scratch_shapes=[pltpu.SemaphoreType.DMA((len(shapes) + 2,))],
        compiler_params=pltpu.CompilerParams(vmem_limit_bytes=VMEM),
    )(row, *arrays)


def target_kernel(
    place_ref, patch_ref, block_ref, level_ref, table_ref, home_ref, *refs, tiles
):
    large_refs = refs[:4]
    slots_ref, own_ref, weights_ref, denom_ref = refs[5:9]
    kept_refs, sems = refs[9:13], refs[13]
    mine, core = place_ref[0], place_ref[1] & 1
    visits, detectors = level_ref.shape
    pieces = slots_ref.shape[0]
    half = weights_ref.shape[0]
    first = mine * (half * 2)
    copies = [
        pltpu.make_async_copy(large.at[pl.ds(core * half, half)], kept, sems.at[i])
        for i, (large, kept) in enumerate(zip(large_refs, kept_refs))
    ]
    for copy in copies:
        copy.start()

    def slot_of(n):
        return (home_ref[patch_ref[n]] ^ mine) * tiles + block_ref[n]

    def place(i, _):
        slots_ref[i] = slot_of(mine * pieces + i)
        return 0

    def place_own(i, _):
        own_ref[i] = slots_ref[core * half * tiles + i]
        return 0

    def weigh(i, _):
        image = first + core * half + i
        weights_ref[i] = table_ref[level_ref[image % visits, image // visits]]
        return 0

    def add(d, sums):
        for v in range(visits):
            weight = table_ref[level_ref[v, d]]
            for q in range(tiles):
                slot = slot_of((d * visits + v) * tiles + q)
                sums = tuple(
                    total + jnp.where(slot == t, weight, 0.0) for t, total in enumerate(sums)
                )
        return sums

    lax.fori_loop(0, pieces, place, 0)
    lax.fori_loop(0, half * tiles, place_own, 0)
    lax.fori_loop(0, half, weigh, 0)
    sums = lax.fori_loop(0, detectors, add, (jnp.float32(0),) * tiles)
    for t in range(tiles):
        denom_ref[t] = sums[t]
    for copy in copies:
        copy.wait()


def match_kernel(slot_ref, weight_ref, row_ref, *refs, start, count, taps, halves, first, warp, send):
    profile_ref, refs = refs[0], refs[1:]
    if warp:
        pixels_ref, rows_ref, cols_ref, passed_ref, passed_rows_ref, far_ref, cross_ref, edge_ref = refs[:8]
        refs = refs[8:]
    else:
        warped_ref, refs = refs[0], refs[1:]
    if not first:
        refs = refs[2 * len(halves) :]
    matched_refs = dict(zip(halves, refs))
    refs = refs[len(halves) :]
    numers = dict(zip(halves, refs))
    refs = refs[len(halves) :]
    if send:
        sent_ref, warped_ref, refs = refs[0], refs[1], refs[2:]
    elif warp:
        warped_ref, refs = refs[-1], refs[:-1]
    tables, refs = refs[:count], refs[count:]
    stacks = {m: refs[count * i : count * (i + 1)] for i, m in enumerate(halves)}
    refs = refs[count * len(halves) :]
    _, band, side = matched_refs[halves[0]].shape
    pad = (warped_ref.shape[1] - 2 * band) // 2
    span = BLOCK + 2 * pad
    reach = (taps - 1) // 2
    inner = DEPTH // span
    outer = -(-taps // inner)
    tiles = side // TILE
    width = side + TILE
    blocks = band // BLOCK
    row = row_ref[0]
    core = row & 1

    if first:
        for numer in numers.values():
            numer[...] = jnp.zeros_like(numer)
    if warp:
        for g in range(count):
            image, extended = refs[g], refs[count + g]
            index = start + g
            there = core * pixels_ref.shape[0] + index
            shards = (pixels_ref.at[index], passed_ref.at[there])
            for mask, shard in enumerate(shards + (far_ref.at[g], cross_ref.at[g])):
                at = pl.multiple_of((row ^ mask) * band, band)
                image[pl.ds(at, band), :] = shard[...]
            edge = edge_ref[index]
            blank = jnp.zeros_like(edge)
            extended[0:pad, :] = jnp.where(row >= 2, edge, blank)
            extended[pad + 2 * band :, :] = jnp.where(row >= 2, blank, edge)
            for which, rows in enumerate((rows_ref.at[index], passed_rows_ref.at[there])):
                at = pl.multiple_of(pad + (core ^ which) * band, ALIGN)
                extended[pl.ds(at, band), :] = rows[...]
    for g in range(count):
        profiles = None
        for b in range(inner):
            part = profile_ref[start + g, pl.ds(b, outer, stride=inner), :]
            part = jnp.concatenate([part, jnp.zeros((outer, DEPTH - TILE), F32)], axis=1)
            part = pltpu.roll(part, span * b, 1) if b else part
            profiles = part if profiles is None else profiles + part
        for a in range(outer):
            profile = jnp.broadcast_to(profiles[a : a + 1, :], (BLOCK, DEPTH))
            toeplitz = pltpu.roll(profile, 0, 1, stride=1, stride_axis=0)
            tables[g][BLOCK * a : BLOCK * (a + 1), :] = toeplitz.astype(BF16)
    for g in range(count):
        if warp:
            image, extended = refs[g], refs[count + g]
            by_rows = jnp.dot(extended[...], image[...], preferred_element_type=F32).astype(BF16)
            warped = jnp.dot(by_rows, cols_ref[start + g], preferred_element_type=F32)
            warped_ref[g] = warped.astype(BF16)
        for m in halves:
            at = pl.multiple_of((core ^ m) * band, band)
            ring = warped_ref[g, pl.ds(at, band + 2 * pad), :]
            ring = jnp.concatenate([ring, jnp.zeros((band + 2 * pad, TILE), BF16)], axis=1)
            stack = stacks[m][g]
            stack[:, span * inner :, :] = jnp.zeros((blocks, DEPTH - span * inner, width), BF16)
            for b in range(inner):
                turn = (inner // 2 - b) % width
                shifted = pltpu.roll(ring, turn, 1) if turn else ring
                for k in range(blocks):
                    stack[k, span * b : span * (b + 1), :] = shifted[BLOCK * k : BLOCK * k + span]
    middle = outer // 2
    origin = inner * middle + inner // 2 - reach
    for m in halves:
        for g in range(count):
            index = start + g
            weight = weight_ref[index]
            for k in range(blocks):
                partial = jnp.dot(tables[g][...], stacks[m][g][k], preferred_element_type=F32)
                total = None
                for a in range(outer):
                    turn = (inner * (middle - a) - origin) % width
                    part = partial[BLOCK * a : BLOCK * (a + 1)]
                    part = pltpu.roll(part, turn, 1) if turn else part
                    total = part if total is None else total + part
                matched = total[:, 0:side]
                here = slice(BLOCK * k, BLOCK * (k + 1))
                matched_refs[m][index, here, :] = matched
                for q in range(tiles):
                    slot = slot_ref[index * tiles + q]
                    piece = (weight * matched[:, TILE * q : TILE * (q + 1)]).astype(BF16)
                    numers[m][slot, here, :] += piece.astype(F32)
    if send:
        sent_ref[...] = numers[1][...].astype(BF16)


def match_chunk(scalars, profiles, operands, carry, start, count, taps, slot_count, halves, send=False):
    warp = len(operands) > 1
    if warp:
        half, band, side = operands[0].shape
        tall = 2 * band + 2 * operands[-1].shape[1]
    else:
        _, tall, side = operands[0].shape
        half, band, _ = carry[0].shape
    inner = DEPTH // (BLOCK + tall - 2 * band)
    outer = -(-taps // inner)
    width = side + TILE
    blocks = band // BLOCK
    first = carry is None
    in_vmem = pl.BlockSpec(memory_space=pltpu.VMEM)
    arrays = list(scalars) + [profiles] + list(operands)
    in_specs = [pl.BlockSpec(memory_space=pltpu.SMEM)] * 3 + [in_vmem] * (len(operands) + 1)
    aliases = {}
    if not first:
        aliases = {len(arrays) + i: i for i in range(len(carry))}
        arrays += list(carry)
        in_specs += [in_vmem] * len(carry)
    matched = jax.ShapeDtypeStruct((half, band, side), F32)
    numer_shape = (slot_count, band, TILE)
    out_shape = [matched] * len(halves) + [jax.ShapeDtypeStruct(numer_shape, F32)] * len(halves)
    if send:
        out_shape.append(jax.ShapeDtypeStruct(numer_shape, BF16))
        out_shape.append(jax.ShapeDtypeStruct((count, tall, side), BF16))
    scratch = [pltpu.VMEM((outer * BLOCK, DEPTH), BF16)] * count
    scratch += [pltpu.VMEM((blocks, DEPTH, width), BF16)] * (count * len(halves))
    if warp:
        scratch += [pltpu.VMEM((side, side), BF16)] * count
        scratch += [pltpu.VMEM((tall, side), BF16)] * count
        if not send:
            scratch.append(pltpu.VMEM((count, tall, side), BF16))
    return pl.pallas_call(
        functools.partial(
            match_kernel,
            start=start,
            count=count,
            taps=taps,
            halves=halves,
            first=first,
            warp=warp,
            send=send,
        ),
        in_specs=in_specs,
        out_specs=[in_vmem] * len(out_shape),
        scratch_shapes=scratch,
        out_shape=out_shape,
        input_output_aliases=aliases,
        compiler_params=pltpu.CompilerParams(vmem_limit_bytes=VMEM),
        cost_estimate=pl.CostEstimate(
            flops=count * 1000000000 * len(halves), bytes_accessed=count * 1000000, transcendentals=0
        ),
    )(*arrays)


def merge_kernel(own_ref, other_ref, *part_refs):
    each = part_refs[0].shape[0]
    for m, part in enumerate(part_refs):
        boxes = slice(each * m, each * (m + 1))
        part[...] = (own_ref[boxes] + other_ref[boxes].astype(F32)).astype(part.dtype)


def add_kernel(own_ref, other_ref, total_ref):
    total_ref[...] = (own_ref[...] + other_ref[...].astype(F32)).astype(BF16)


def template_kernel(denom_ref, _, *refs):
    part_refs, template_ref = refs[:-2], refs[-2]
    for q in range(template_ref.shape[0]):
        total = part_refs[0][q].astype(F32)
        for part in part_refs[1:]:
            total = total + part[q].astype(F32)
        box = (total / jnp.maximum(denom_ref[q], 1.0)).astype(BF16)
        template_ref[q] = box


def coadd_kernel(template_ref, coadd_ref):
    for q in range(template_ref.shape[0]):
        coadd_ref[:, TILE * q : TILE * (q + 1)] = template_ref[q]


def difference_kernel(slot_ref, row_ref, own_ref, other_ref, *refs, group, masks):
    template_refs, out_ref = refs[:-4], refs[-4]
    held, ready, sems = refs[-3:]
    each = template_refs[0].shape[0]
    half, _, side = own_ref.shape
    tiles = side // TILE
    core = row_ref[0] & 1
    for m, template in zip(masks, template_refs):
        held[each * m : each * (m + 1)] = template[...]
    copies = []
    for which, matched_ref in enumerate((own_ref, other_ref)):
        for first in range(0, half, group):
            at = (core ^ which) * half + first
            for i in range(group):
                for q in range(tiles):
                    slot = slot_ref[(at + i) * tiles + q]
                    columns = slice(TILE * q, TILE * (q + 1))
                    box = held[slot].astype(F32)
                    value = (matched_ref[first + i, :, columns] - box).astype(BF16)
                    ready[which * half + first + i, :, columns] = value
            copies.append(
                pltpu.make_async_copy(
                    ready.at[pl.ds(which * half + first, group)],
                    out_ref.at[pl.ds(at, group)],
                    sems.at[len(copies)],
                )
            )
            copies[-1].start()
    for copy in copies:
        copy.wait()


def exchange(value, axis, mask):
    size = lax.axis_size(axis)
    return lax.ppermute(value, axis, [(i, i ^ mask) for i in range(size)])


def per_device(
    images,
    warp_rows,
    warp_cols,
    psf_coef,
    taps,
    dest_patch,
    dest_block,
    weight_index,
    weight_table,
    patch_home,
):
    det_count, visit_count, band, side = images.shape
    kernel_count, tap_count = taps.shape
    reach = (tap_count - 1) // 2
    pad = -(-reach // ALIGN) * ALIGN
    span = BLOCK + 2 * pad
    tiles = side // TILE
    det_devices = lax.axis_size("det")
    mine = lax.axis_index("det")
    row = lax.axis_index("row").astype(jnp.int32)
    core = row & 1
    image_count = det_count * visit_count
    half = image_count // 2
    assert lax.axis_size("row") == 4 and image_count == 2 * half
    pixels = images.reshape(image_count, band, side)
    rows = warp_rows.reshape(image_count, band, side)
    cols = warp_cols.reshape(image_count, side, side)
    row_one = row.reshape(1)

    chunks = CHUNKS if sum(CHUNKS) == half else (1,) * half
    starts = [sum(chunks[:c]) for c in range(len(chunks))]
    spans = list(zip(starts, chunks))
    far, cross = [], []

    def send(packed):
        for first, second in zip(packed[::2], packed[1::2]):
            far.append(exchange(first, "row", 2))
            cross.append(exchange(second, "row", 3))

    send(pack(row_one, pixels, rows, spans[:1], pad))
    sibling_rows = exchange(rows, "row", 1)
    sibling_pixels = exchange(pixels, "row", 1)
    packed = pack(row_one, pixels, rows, spans[-1:], pad, sibling_rows=sibling_rows)
    edge = exchange(packed[-1], "row", 2)
    send(pack(row_one, pixels, rows, spans[1:-1], pad, after=[far[0]]))
    send(packed[:-1])

    with jax.named_scope("profiles"):
        scaled = (psf_coef.reshape(image_count, kernel_count)[:, :, None] * taps).astype(BF16)
        profiles = jnp.einsum(
            "nkt,ku->nut", scaled, taps.astype(BF16), preferred_element_type=F32
        )
        inner = DEPTH // span
        rows_kept = -(-tap_count // inner) * inner
        profiles = jnp.pad(
            profiles,
            (
                (0, 0),
                (0, rows_kept - tap_count + -rows_kept % 8),
                (pad - reach, TILE - tap_count - pad + reach),
            ),
        )
    anywhere = pl.BlockSpec(memory_space=pl.ANY)
    in_vmem = pl.BlockSpec(memory_space=pltpu.VMEM)
    large = (pixels, rows, cols, profiles)
    slots, own_slots, weights, denom, *kept = pl.pallas_call(
        functools.partial(target_kernel, tiles=tiles),
        in_specs=[pl.BlockSpec(memory_space=pltpu.SMEM)] * 6 + [anywhere] * 5,
        out_specs=[pl.BlockSpec(memory_space=pltpu.SMEM)] * 4 + [in_vmem] * 4,
        out_shape=[
            jax.ShapeDtypeStruct((image_count * tiles,), jnp.int32),
            jax.ShapeDtypeStruct((half * tiles,), jnp.int32),
            jax.ShapeDtypeStruct((half,), F32),
            jax.ShapeDtypeStruct((tiles,), F32),
        ]
        + [jax.ShapeDtypeStruct((half,) + a.shape[1:], a.dtype) for a in large],
        scratch_shapes=[pltpu.SemaphoreType.DMA((len(large),))],
        compiler_params=pltpu.CompilerParams(vmem_limit_bytes=VMEM),
    )(
        jnp.stack([mine.astype(jnp.int32), row]),
        dest_patch.reshape(-1),
        dest_block,
        weight_index.T,
        weight_table,
        patch_home,
        *[pltpu.with_memory_space_constraint(a, pltpu.HBM) for a in large],
        packed[-1],
    )

    carry = None
    slot_count = det_devices * tiles
    scalars = (own_slots, weights, row_one)
    common = (tap_count, slot_count)
    for c, (s, n) in enumerate(spans):
        operands = tuple(kept[:3]) + (sibling_pixels, sibling_rows, far[c], cross[c], edge)
        if c < len(spans) - 1:
            carry = match_chunk(scalars, kept[3], operands, carry, s, n, *common, (0, 1))
    matched_sent, _, sums_sent, warped = match_chunk(
        scalars, kept[3], operands, carry[1::2], s, n, *common, (1,), send=True
    )
    other_sums = exchange(sums_sent, "row", 1)
    matched, own_sums = match_chunk(
        scalars, kept[3], (warped,), carry[0::2], s, n, *common, (0,)
    )
    box_shape = (tiles, band, TILE)
    box = jax.ShapeDtypeStruct(box_shape, BF16)
    small = pltpu.CompilerParams(vmem_limit_bytes=4 * MIB + 16 * slot_count * band * TILE)
    parts = pl.pallas_call(
        merge_kernel,
        in_specs=[in_vmem] * 2,
        out_specs=[in_vmem] * det_devices,
        out_shape=[
            jax.ShapeDtypeStruct(box_shape, BF16 if m % 2 else F32) for m in range(det_devices)
        ],
        compiler_params=small,
    )(own_sums, other_sums)
    evens = tuple(range(2, det_devices, 2))
    across = {m: exchange(parts[m ^ 1], "det", 1) for m in evens + (0,)}
    received = [parts[0], across[0]]
    for m in evens:
        total = pl.pallas_call(
            add_kernel,
            in_specs=[in_vmem] * 2,
            out_specs=in_vmem,
            out_shape=box,
            compiler_params=small,
        )(parts[m], across[m])
        received.append(exchange(total, "det", m))
    template, matched_sent = pl.pallas_call(
        template_kernel,
        in_specs=[pl.BlockSpec(memory_space=pltpu.SMEM), anywhere] + [in_vmem] * len(received),
        out_specs=[in_vmem, anywhere],
        out_shape=[
            box,
            jax.ShapeDtypeStruct(matched_sent.shape, F32),
        ],
        input_output_aliases={1: 1},
        compiler_params=small,
    )(denom, matched_sent, *received)
    other_matched = exchange(matched_sent, "row", 1)
    passed = {0: template}
    for m in evens:
        passed[m] = exchange(template, "det", m)
    for m in evens + (0,):
        passed[m ^ 1] = exchange(passed[m], "det", 1)
    masks = tuple(range(det_devices - 1, -1, -1))
    templates = [passed[m] for m in masks]
    coadd = pl.pallas_call(
        coadd_kernel,
        in_specs=[in_vmem],
        out_specs=in_vmem,
        out_shape=jax.ShapeDtypeStruct((band, side), BF16),
        compiler_params=small,
    )(template)
    group = 3 if half % 3 == 0 else 1
    difference = pl.pallas_call(
        functools.partial(difference_kernel, group=group, masks=masks),
        in_specs=[pl.BlockSpec(memory_space=pltpu.SMEM)] * 2 + [in_vmem] * (2 + det_devices),
        out_specs=anywhere,
        scratch_shapes=[
            pltpu.VMEM((slot_count, band, TILE), BF16),
            pltpu.VMEM((image_count, band, side), BF16),
            pltpu.SemaphoreType.DMA((image_count // group,)),
        ],
        out_shape=jax.ShapeDtypeStruct((image_count, band, side), BF16),
        compiler_params=small,
    )(slots, row_one, matched, other_matched, *templates)
    return difference.reshape(images.shape), coadd.reshape(1, band, side)


def solution(mesh):
    placed = (
        P("det", None, "row", None),
        P("det", None, "row", None),
        P("det", None, None, None),
        P("det", None, None),
        P(),
        P(),
        P(),
        P(),
        P(),
        P(),
    )
    return jax.shard_map(
        per_device,
        mesh=mesh,
        in_specs=placed,
        out_specs=(P("det", None, "row", None), P("det", "row", None)),
        check_vma=False,
    )
```

```python
import functools

import jax
import jax.numpy as jnp
from jax import lax
from jax.experimental import pallas as pl
from jax.experimental.pallas import tpu as pltpu
from jax.sharding import PartitionSpec as P

TILE = 128
ALIGN = 16
CHUNKS = (3, 4, 2)
BLOCK = 32
DEPTH = 256
MIB = 1024 * 1024
VMEM = 20 * MIB
F32 = jnp.float32
BF16 = jnp.bfloat16


def pack_kernel(row_ref, *refs, chunks, edges):
    sems = refs[-1]
    outs = list(refs[-1 - 2 * len(chunks) - edges : -1])
    pixels_ref, rows_ref = refs[:2]
    half = pixels_ref.shape[0] // 2
    row = row_ref[0]
    core = row & 1
    pieces = []
    for s, n in chunks:
        for which in range(2):
            pieces.append(pixels_ref.at[pl.ds((core ^ which) * half + s, n)])
    copies = [
        pltpu.make_async_copy(piece, out, sems.at[i]) for i, (piece, out) in enumerate(zip(pieces, outs))
    ]
    for copy in copies:
        copy.start()
    if edges:
        pad = outs[-1].shape[1]
        first = jnp.where(row < 2, rows_ref.shape[1] - pad, 0)
        near = pl.ds(pl.multiple_of(first, ALIGN), pad)
        holds = core == (row < 2).astype(jnp.int32)
        own = rows_ref.at[pl.ds(core * half, half), near]
        edge = pltpu.make_async_copy(own, outs[-1], sems.at[len(pieces)])
        passed = pltpu.make_async_copy(
            refs[2].at[pl.ds(core * half, half), near], outs[-1], sems.at[len(pieces)]
        )
        pl.when(holds)(edge.start)
        pl.when(jnp.logical_not(holds))(passed.start)
        copies.append(edge)
    for copy in copies:
        copy.wait()


def pack(row, pixels, rows, chunks, pad, sibling_rows=None, after=()):
    images, band, side = pixels.shape
    half = images // 2
    shapes = [(n, band, side) for _, n in chunks for _ in range(2)]
    arrays = [pltpu.with_memory_space_constraint(a, pltpu.HBM) for a in (pixels, rows)]
    if sibling_rows is not None:
        shapes.append((half, pad, side))
        arrays.append(sibling_rows)
    arrays += after
    anywhere = pl.BlockSpec(memory_space=pl.ANY)
    return pl.pallas_call(
        functools.partial(
            pack_kernel, chunks=chunks, edges=sibling_rows is not None
        ),
        in_specs=[pl.BlockSpec(memory_space=pltpu.SMEM)] + [anywhere] * len(arrays),
        out_specs=[pl.BlockSpec(memory_space=pltpu.VMEM)] * len(shapes),
        out_shape=[jax.ShapeDtypeStruct(shape, BF16) for shape in shapes],
        scratch_shapes=[pltpu.SemaphoreType.DMA((len(shapes) + 2,))],
        compiler_params=pltpu.CompilerParams(vmem_limit_bytes=VMEM),
    )(row, *arrays)


def target_kernel(
    place_ref, patch_ref, block_ref, level_ref, table_ref, home_ref, *refs, tiles
):
    large_refs = refs[:4]
    slots_ref, own_ref, weights_ref, denom_ref = refs[5:9]
    kept_refs, sems = refs[9:13], refs[13]
    mine, core = place_ref[0], place_ref[1] & 1
    visits, detectors = level_ref.shape
    pieces = slots_ref.shape[0]
    half = weights_ref.shape[0]
    first = mine * (half * 2)
    copies = [
        pltpu.make_async_copy(large.at[pl.ds(core * half, half)], kept, sems.at[i])
        for i, (large, kept) in enumerate(zip(large_refs, kept_refs))
    ]
    for copy in copies:
        copy.start()

    def slot_of(n):
        return (home_ref[patch_ref[n]] ^ mine) * tiles + block_ref[n]

    def place(i, _):
        slots_ref[i] = slot_of(mine * pieces + i)
        return 0

    def place_own(i, _):
        own_ref[i] = slots_ref[core * half * tiles + i]
        return 0

    def weigh(i, _):
        image = first + core * half + i
        weights_ref[i] = table_ref[level_ref[image % visits, image // visits]]
        return 0

    def add(d, sums):
        for v in range(visits):
            weight = table_ref[level_ref[v, d]]
            for q in range(tiles):
                slot = slot_of((d * visits + v) * tiles + q)
                sums = tuple(
                    total + jnp.where(slot == t, weight, 0.0) for t, total in enumerate(sums)
                )
        return sums

    lax.fori_loop(0, pieces, place, 0)
    lax.fori_loop(0, half * tiles, place_own, 0)
    lax.fori_loop(0, half, weigh, 0)
    sums = lax.fori_loop(0, detectors, add, (jnp.float32(0),) * tiles)
    for t in range(tiles):
        denom_ref[t] = sums[t]
    for copy in copies:
        copy.wait()


def match_kernel(slot_ref, weight_ref, row_ref, *refs, start, count, taps, halves, first, warp, send):
    profile_ref, refs = refs[0], refs[1:]
    if warp:
        pixels_ref, rows_ref, cols_ref, passed_ref, passed_rows_ref, far_ref, cross_ref, edge_ref = refs[:8]
        refs = refs[8:]
    else:
        warped_ref, refs = refs[0], refs[1:]
    if not first:
        refs = refs[2 * len(halves) :]
    matched_refs = dict(zip(halves, refs))
    refs = refs[len(halves) :]
    numers = dict(zip(halves, refs))
    refs = refs[len(halves) :]
    if send:
        sent_ref, warped_ref, refs = refs[0], refs[1], refs[2:]
    elif warp:
        warped_ref, refs = refs[-1], refs[:-1]
    tables, refs = refs[:count], refs[count:]
    stacks = {m: refs[count * i : count * (i + 1)] for i, m in enumerate(halves)}
    refs = refs[count * len(halves) :]
    _, band, side = matched_refs[halves[0]].shape
    pad = (warped_ref.shape[1] - 2 * band) // 2
    span = BLOCK + 2 * pad
    reach = (taps - 1) // 2
    inner = DEPTH // span
    outer = -(-taps // inner)
    tiles = side // TILE
    width = side + TILE
    blocks = band // BLOCK
    row = row_ref[0]
    core = row & 1

    if first:
        for numer in numers.values():
            numer[...] = jnp.zeros_like(numer)
    if warp:
        for g in range(count):
            image, extended = refs[g], refs[count + g]
            index = start + g
            there = core * pixels_ref.shape[0] + index
            shards = (pixels_ref.at[index], passed_ref.at[there])
            for mask, shard in enumerate(shards + (far_ref.at[g], cross_ref.at[g])):
                at = pl.multiple_of((row ^ mask) * band, band)
                image[pl.ds(at, band), :] = shard[...]
            edge = edge_ref[index]
            blank = jnp.zeros_like(edge)
            extended[0:pad, :] = jnp.where(row >= 2, edge, blank)
            extended[pad + 2 * band :, :] = jnp.where(row >= 2, blank, edge)
            for which, rows in enumerate((rows_ref.at[index], passed_rows_ref.at[there])):
                at = pl.multiple_of(pad + (core ^ which) * band, ALIGN)
                extended[pl.ds(at, band), :] = rows[...]
    for g in range(count):
        profiles = None
        for b in range(inner):
            part = profile_ref[start + g, pl.ds(b, outer, stride=inner), :]
            part = jnp.concatenate([part, jnp.zeros((outer, DEPTH - TILE), F32)], axis=1)
            part = pltpu.roll(part, span * b, 1) if b else part
            profiles = part if profiles is None else profiles + part
        for a in range(outer):
            profile = jnp.broadcast_to(profiles[a : a + 1, :], (BLOCK, DEPTH))
            toeplitz = pltpu.roll(profile, 0, 1, stride=1, stride_axis=0)
            tables[g][BLOCK * a : BLOCK * (a + 1), :] = toeplitz.astype(BF16)
    for g in range(count):
        if warp:
            image, extended = refs[g], refs[count + g]
            by_rows = jnp.dot(extended[...], image[...], preferred_element_type=F32).astype(BF16)
            warped = jnp.dot(by_rows, cols_ref[start + g], preferred_element_type=F32)
            warped_ref[g] = warped.astype(BF16)
        for m in halves:
            at = pl.multiple_of((core ^ m) * band, band)
            ring = warped_ref[g, pl.ds(at, band + 2 * pad), :]
            ring = jnp.concatenate([ring, jnp.zeros((band + 2 * pad, TILE), BF16)], axis=1)
            stack = stacks[m][g]
            if span * inner < DEPTH:
                rest = (blocks, DEPTH - span * inner, width)
                stack[:, span * inner :, :] = jnp.zeros(rest, BF16)
            for b in range(inner):
                turn = (inner // 2 - b) % width
                shifted = pltpu.roll(ring, turn, 1) if turn else ring
                for k in range(blocks):
                    stack[k, span * b : span * (b + 1), :] = shifted[BLOCK * k : BLOCK * k + span]
    middle = outer // 2
    origin = inner * middle + inner // 2 - reach
    for m in halves:
        for g in range(count):
            index = start + g
            weight = weight_ref[index]
            for k in range(blocks):
                partial = jnp.dot(tables[g][...], stacks[m][g][k], preferred_element_type=F32)
                total = None
                for a in range(outer):
                    turn = (inner * (middle - a) - origin) % width
                    part = partial[BLOCK * a : BLOCK * (a + 1)]
                    part = pltpu.roll(part, turn, 1) if turn else part
                    total = part if total is None else total + part
                matched = total[:, 0:side]
                here = slice(BLOCK * k, BLOCK * (k + 1))
                matched_refs[m][index, here, :] = matched
                for q in range(tiles):
                    slot = slot_ref[index * tiles + q]
                    piece = (weight * matched[:, TILE * q : TILE * (q + 1)]).astype(BF16)
                    numers[m][slot, here, :] += piece.astype(F32)
    if send:
        sent_ref[...] = numers[1][...].astype(BF16)


def match_chunk(scalars, profiles, operands, carry, start, count, taps, slot_count, halves, send=False):
    warp = len(operands) > 1
    if warp:
        half, band, side = operands[0].shape
        tall = 2 * band + 2 * operands[-1].shape[1]
    else:
        _, tall, side = operands[0].shape
        half, band, _ = carry[0].shape
    inner = DEPTH // (BLOCK + tall - 2 * band)
    outer = -(-taps // inner)
    width = side + TILE
    blocks = band // BLOCK
    first = carry is None
    in_vmem = pl.BlockSpec(memory_space=pltpu.VMEM)
    arrays = list(scalars) + [profiles] + list(operands)
    in_specs = [pl.BlockSpec(memory_space=pltpu.SMEM)] * 3 + [in_vmem] * (len(operands) + 1)
    aliases = {}
    if not first:
        aliases = {len(arrays) + i: i for i in range(len(carry))}
        arrays += list(carry)
        in_specs += [in_vmem] * len(carry)
    matched = jax.ShapeDtypeStruct((half, band, side), F32)
    numer_shape = (slot_count, band, TILE)
    out_shape = [matched] * len(halves) + [jax.ShapeDtypeStruct(numer_shape, F32)] * len(halves)
    if send:
        out_shape.append(jax.ShapeDtypeStruct(numer_shape, BF16))
        out_shape.append(jax.ShapeDtypeStruct((count, tall, side), BF16))
    scratch = [pltpu.VMEM((outer * BLOCK, DEPTH), BF16)] * count
    scratch += [pltpu.VMEM((blocks, DEPTH, width), BF16)] * (count * len(halves))
    if warp:
        scratch += [pltpu.VMEM((side, side), BF16)] * count
        scratch += [pltpu.VMEM((tall, side), BF16)] * count
        if not send:
            scratch.append(pltpu.VMEM((count, tall, side), BF16))
    return pl.pallas_call(
        functools.partial(
            match_kernel,
            start=start,
            count=count,
            taps=taps,
            halves=halves,
            first=first,
            warp=warp,
            send=send,
        ),
        in_specs=in_specs,
        out_specs=[in_vmem] * len(out_shape),
        scratch_shapes=scratch,
        out_shape=out_shape,
        input_output_aliases=aliases,
        compiler_params=pltpu.CompilerParams(vmem_limit_bytes=VMEM),
        cost_estimate=pl.CostEstimate(
            flops=count * 1000000000 * len(halves), bytes_accessed=count * 1000000, transcendentals=0
        ),
    )(*arrays)


def merge_kernel(own_ref, other_ref, *part_refs):
    each = part_refs[0].shape[0]
    for m, part in enumerate(part_refs):
        boxes = slice(each * m, each * (m + 1))
        part[...] = (own_ref[boxes] + other_ref[boxes].astype(F32)).astype(part.dtype)


def add_kernel(own_ref, other_ref, total_ref):
    total_ref[...] = (own_ref[...] + other_ref[...].astype(F32)).astype(BF16)


def template_kernel(denom_ref, _, *refs):
    part_refs, template_ref = refs[:-2], refs[-2]
    for q in range(template_ref.shape[0]):
        total = part_refs[0][q].astype(F32)
        for part in part_refs[1:]:
            total = total + part[q].astype(F32)
        box = (total / jnp.maximum(denom_ref[q], 1.0)).astype(BF16)
        template_ref[q] = box


def coadd_kernel(template_ref, coadd_ref):
    for q in range(template_ref.shape[0]):
        coadd_ref[:, TILE * q : TILE * (q + 1)] = template_ref[q]


def difference_kernel(slot_ref, row_ref, own_ref, other_ref, *refs, group, masks):
    template_refs, out_ref = refs[:-4], refs[-4]
    held, ready, sems = refs[-3:]
    each = template_refs[0].shape[0]
    half, _, side = own_ref.shape
    tiles = side // TILE
    core = row_ref[0] & 1
    for m, template in zip(masks, template_refs):
        held[each * m : each * (m + 1)] = template[...]
    copies = []
    for which, matched_ref in enumerate((own_ref, other_ref)):
        for first in range(0, half, group):
            at = (core ^ which) * half + first
            for i in range(group):
                for q in range(tiles):
                    slot = slot_ref[(at + i) * tiles + q]
                    columns = slice(TILE * q, TILE * (q + 1))
                    box = held[slot].astype(F32)
                    value = (matched_ref[first + i, :, columns] - box).astype(BF16)
                    ready[which * half + first + i, :, columns] = value
            copies.append(
                pltpu.make_async_copy(
                    ready.at[pl.ds(which * half + first, group)],
                    out_ref.at[pl.ds(at, group)],
                    sems.at[len(copies)],
                )
            )
            copies[-1].start()
    for copy in copies:
        copy.wait()


def exchange(value, axis, mask):
    size = lax.axis_size(axis)
    return lax.ppermute(value, axis, [(i, i ^ mask) for i in range(size)])


def per_device(
    images,
    warp_rows,
    warp_cols,
    psf_coef,
    taps,
    dest_patch,
    dest_block,
    weight_index,
    weight_table,
    patch_home,
):
    det_count, visit_count, band, side = images.shape
    kernel_count, tap_count = taps.shape
    reach = (tap_count - 1) // 2
    pad = -(-reach // ALIGN) * ALIGN
    span = BLOCK + 2 * pad
    tiles = side // TILE
    det_devices = lax.axis_size("det")
    mine = lax.axis_index("det")
    row = lax.axis_index("row").astype(jnp.int32)
    core = row & 1
    image_count = det_count * visit_count
    half = image_count // 2
    assert lax.axis_size("row") == 4 and image_count == 2 * half
    pixels = images.reshape(image_count, band, side)
    rows = warp_rows.reshape(image_count, band, side)
    cols = warp_cols.reshape(image_count, side, side)
    row_one = row.reshape(1)

    chunks = CHUNKS if sum(CHUNKS) == half else (1,) * half
    starts = [sum(chunks[:c]) for c in range(len(chunks))]
    spans = list(zip(starts, chunks))
    far, cross = [], []

    def send(packed):
        for first, second in zip(packed[::2], packed[1::2]):
            far.append(exchange(first, "row", 2))
            cross.append(exchange(second, "row", 3))

    send(pack(row_one, pixels, rows, spans[:1], pad))
    sibling_rows = exchange(rows, "row", 1)
    sibling_pixels = exchange(pixels, "row", 1)
    packed = pack(row_one, pixels, rows, spans[-1:], pad, sibling_rows=sibling_rows)
    edge = exchange(packed[-1], "row", 2)
    send(pack(row_one, pixels, rows, spans[1:-1], pad, after=[far[0]]))
    send(packed[:-1])

    with jax.named_scope("profiles"):
        scaled = (psf_coef.reshape(image_count, kernel_count)[:, :, None] * taps).astype(BF16)
        profiles = jnp.einsum(
            "nkt,ku->nut", scaled, taps.astype(BF16), preferred_element_type=F32
        )
        inner = DEPTH // span
        rows_kept = -(-tap_count // inner) * inner
        profiles = jnp.pad(
            profiles,
            (
                (0, 0),
                (0, rows_kept - tap_count + -rows_kept % 8),
                (pad - reach, TILE - tap_count - pad + reach),
            ),
        )
    anywhere = pl.BlockSpec(memory_space=pl.ANY)
    in_vmem = pl.BlockSpec(memory_space=pltpu.VMEM)
    large = (pixels, rows, cols, profiles)
    slots, own_slots, weights, denom, *kept = pl.pallas_call(
        functools.partial(target_kernel, tiles=tiles),
        in_specs=[pl.BlockSpec(memory_space=pltpu.SMEM)] * 6 + [anywhere] * 5,
        out_specs=[pl.BlockSpec(memory_space=pltpu.SMEM)] * 4 + [in_vmem] * 4,
        out_shape=[
            jax.ShapeDtypeStruct((image_count * tiles,), jnp.int32),
            jax.ShapeDtypeStruct((half * tiles,), jnp.int32),
            jax.ShapeDtypeStruct((half,), F32),
            jax.ShapeDtypeStruct((tiles,), F32),
        ]
        + [jax.ShapeDtypeStruct((half,) + a.shape[1:], a.dtype) for a in large],
        scratch_shapes=[pltpu.SemaphoreType.DMA((len(large),))],
        compiler_params=pltpu.CompilerParams(vmem_limit_bytes=VMEM),
    )(
        jnp.stack([mine.astype(jnp.int32), row]),
        dest_patch.reshape(-1),
        dest_block,
        weight_index.T,
        weight_table,
        patch_home,
        *[pltpu.with_memory_space_constraint(a, pltpu.HBM) for a in large],
        packed[-1],
    )

    carry = None
    slot_count = det_devices * tiles
    scalars = (own_slots, weights, row_one)
    common = (tap_count, slot_count)
    for c, (s, n) in enumerate(spans):
        operands = tuple(kept[:3]) + (sibling_pixels, sibling_rows, far[c], cross[c], edge)
        if c < len(spans) - 1:
            carry = match_chunk(scalars, kept[3], operands, carry, s, n, *common, (0, 1))
    matched_sent, _, sums_sent, warped = match_chunk(
        scalars, kept[3], operands, carry[1::2], s, n, *common, (1,), send=True
    )
    other_sums = exchange(sums_sent, "row", 1)
    matched, own_sums = match_chunk(
        scalars, kept[3], (warped,), carry[0::2], s, n, *common, (0,)
    )
    box_shape = (tiles, band, TILE)
    box = jax.ShapeDtypeStruct(box_shape, BF16)
    small = pltpu.CompilerParams(vmem_limit_bytes=4 * MIB + 16 * slot_count * band * TILE)
    parts = pl.pallas_call(
        merge_kernel,
        in_specs=[in_vmem] * 2,
        out_specs=[in_vmem] * det_devices,
        out_shape=[
            jax.ShapeDtypeStruct(box_shape, BF16 if m % 2 else F32) for m in range(det_devices)
        ],
        compiler_params=small,
    )(own_sums, other_sums)
    evens = tuple(range(2, det_devices, 2))
    across = {m: exchange(parts[m ^ 1], "det", 1) for m in evens + (0,)}
    received = [parts[0], across[0]]
    for m in evens:
        total = pl.pallas_call(
            add_kernel,
            in_specs=[in_vmem] * 2,
            out_specs=in_vmem,
            out_shape=box,
            compiler_params=small,
        )(parts[m], across[m])
        received.append(exchange(total, "det", m))
    template, matched_sent = pl.pallas_call(
        template_kernel,
        in_specs=[pl.BlockSpec(memory_space=pltpu.SMEM), anywhere] + [in_vmem] * len(received),
        out_specs=[in_vmem, anywhere],
        out_shape=[
            box,
            jax.ShapeDtypeStruct(matched_sent.shape, F32),
        ],
        input_output_aliases={1: 1},
        compiler_params=small,
    )(denom, matched_sent, *received)
    other_matched = exchange(matched_sent, "row", 1)
    passed = {0: template}
    for m in evens:
        passed[m] = exchange(template, "det", m)
    for m in evens + (0,):
        passed[m ^ 1] = exchange(passed[m], "det", 1)
    masks = tuple(range(det_devices - 1, -1, -1))
    templates = [passed[m] for m in masks]
    coadd = pl.pallas_call(
        coadd_kernel,
        in_specs=[in_vmem],
        out_specs=in_vmem,
        out_shape=jax.ShapeDtypeStruct((band, side), BF16),
        compiler_params=small,
    )(template)
    group = 3 if half % 3 == 0 else 1
    difference = pl.pallas_call(
        functools.partial(difference_kernel, group=group, masks=masks),
        in_specs=[pl.BlockSpec(memory_space=pltpu.SMEM)] * 2 + [in_vmem] * (2 + det_devices),
        out_specs=anywhere,
        scratch_shapes=[
            pltpu.VMEM((slot_count, band, TILE), BF16),
            pltpu.VMEM((image_count, band, side), BF16),
            pltpu.SemaphoreType.DMA((image_count // group,)),
        ],
        out_shape=jax.ShapeDtypeStruct((image_count, band, side), BF16),
        compiler_params=small,
    )(slots, row_one, matched, other_matched, *templates)
    return difference.reshape(images.shape), coadd.reshape(1, band, side)


def solution(mesh):
    placed = (
        P("det", None, "row", None),
        P("det", None, "row", None),
        P("det", None, None, None),
        P("det", None, None),
        P(),
        P(),
        P(),
        P(),
        P(),
        P(),
    )
    return jax.shard_map(
        per_device,
        mesh=mesh,
        in_specs=placed,
        out_specs=(P("det", None, "row", None), P("det", "row", None)),
        check_vma=False,
    )
```

```python
import functools

import jax
import jax.numpy as jnp
from jax import lax
from jax.experimental import pallas as pl
from jax.experimental.pallas import tpu as pltpu
from jax.sharding import PartitionSpec as P

TILE = 128
ALIGN = 16
CHUNKS = (2, 5, 2)
BLOCK = 32
DEPTH = 256
MIB = 1024 * 1024
VMEM = 20 * MIB
F32 = jnp.float32
BF16 = jnp.bfloat16


def pack_kernel(row_ref, *refs, chunks, edges):
    sems = refs[-1]
    outs = list(refs[-1 - 2 * len(chunks) - edges : -1])
    pixels_ref, rows_ref = refs[:2]
    half = pixels_ref.shape[0] // 2
    row = row_ref[0]
    core = row & 1
    pieces = []
    for s, n in chunks:
        for which in range(2):
            pieces.append(pixels_ref.at[pl.ds((core ^ which) * half + s, n)])
    copies = [
        pltpu.make_async_copy(piece, out, sems.at[i]) for i, (piece, out) in enumerate(zip(pieces, outs))
    ]
    for copy in copies:
        copy.start()
    if edges:
        pad = outs[-1].shape[1]
        first = jnp.where(row < 2, rows_ref.shape[1] - pad, 0)
        near = pl.ds(pl.multiple_of(first, ALIGN), pad)
        holds = core == (row < 2).astype(jnp.int32)
        own = rows_ref.at[pl.ds(core * half, half), near]
        edge = pltpu.make_async_copy(own, outs[-1], sems.at[len(pieces)])
        passed = pltpu.make_async_copy(
            refs[2].at[pl.ds(core * half, half), near], outs[-1], sems.at[len(pieces)]
        )
        pl.when(holds)(edge.start)
        pl.when(jnp.logical_not(holds))(passed.start)
        copies.append(edge)
    for copy in copies:
        copy.wait()


def pack(row, pixels, rows, chunks, pad, sibling_rows=None, after=()):
    images, band, side = pixels.shape
    half = images // 2
    shapes = [(n, band, side) for _, n in chunks for _ in range(2)]
    arrays = [pltpu.with_memory_space_constraint(a, pltpu.HBM) for a in (pixels, rows)]
    if sibling_rows is not None:
        shapes.append((half, pad, side))
        arrays.append(sibling_rows)
    arrays += after
    anywhere = pl.BlockSpec(memory_space=pl.ANY)
    return pl.pallas_call(
        functools.partial(
            pack_kernel, chunks=chunks, edges=sibling_rows is not None
        ),
        in_specs=[pl.BlockSpec(memory_space=pltpu.SMEM)] + [anywhere] * len(arrays),
        out_specs=[pl.BlockSpec(memory_space=pltpu.VMEM)] * len(shapes),
        out_shape=[jax.ShapeDtypeStruct(shape, BF16) for shape in shapes],
        scratch_shapes=[pltpu.SemaphoreType.DMA((len(shapes) + 2,))],
        compiler_params=pltpu.CompilerParams(vmem_limit_bytes=VMEM),
    )(row, *arrays)


def target_kernel(
    place_ref, patch_ref, block_ref, level_ref, table_ref, home_ref, *refs, tiles
):
    large_refs = refs[:4]
    slots_ref, own_ref, weights_ref, denom_ref = refs[5:9]
    kept_refs, sems = refs[9:13], refs[13]
    mine, core = place_ref[0], place_ref[1] & 1
    visits, detectors = level_ref.shape
    pieces = slots_ref.shape[0]
    half = weights_ref.shape[0]
    first = mine * (half * 2)
    copies = [
        pltpu.make_async_copy(large.at[pl.ds(core * half, half)], kept, sems.at[i])
        for i, (large, kept) in enumerate(zip(large_refs, kept_refs))
    ]
    for copy in copies:
        copy.start()

    def slot_of(n):
        return (home_ref[patch_ref[n]] ^ mine) * tiles + block_ref[n]

    def place(i, _):
        slots_ref[i] = slot_of(mine * pieces + i)
        return 0

    def place_own(i, _):
        own_ref[i] = slots_ref[core * half * tiles + i]
        return 0

    def weigh(i, _):
        image = first + core * half + i
        weights_ref[i] = table_ref[level_ref[image % visits, image // visits]]
        return 0

    def add(d, sums):
        for v in range(visits):
            weight = table_ref[level_ref[v, d]]
            for q in range(tiles):
                slot = slot_of((d * visits + v) * tiles + q)
                sums = tuple(
                    total + jnp.where(slot == t, weight, 0.0) for t, total in enumerate(sums)
                )
        return sums

    lax.fori_loop(0, pieces, place, 0)
    lax.fori_loop(0, half * tiles, place_own, 0)
    lax.fori_loop(0, half, weigh, 0)
    sums = lax.fori_loop(0, detectors, add, (jnp.float32(0),) * tiles)
    for t in range(tiles):
        denom_ref[t] = sums[t]
    for copy in copies:
        copy.wait()


def match_kernel(slot_ref, weight_ref, row_ref, *refs, start, count, taps, halves, first, warp, send):
    profile_ref, refs = refs[0], refs[1:]
    if warp:
        pixels_ref, rows_ref, cols_ref, passed_ref, passed_rows_ref, far_ref, cross_ref, edge_ref = refs[:8]
        refs = refs[8:]
    else:
        warped_ref, refs = refs[0], refs[1:]
    if not first:
        refs = refs[2 * len(halves) :]
    matched_refs = dict(zip(halves, refs))
    refs = refs[len(halves) :]
    numers = dict(zip(halves, refs))
    refs = refs[len(halves) :]
    if send:
        sent_ref, warped_ref, refs = refs[0], refs[1], refs[2:]
    elif warp:
        warped_ref, refs = refs[-1], refs[:-1]
    tables, refs = refs[:count], refs[count:]
    stacks = {m: refs[count * i : count * (i + 1)] for i, m in enumerate(halves)}
    refs = refs[count * len(halves) :]
    _, band, side = matched_refs[halves[0]].shape
    pad = (warped_ref.shape[1] - 2 * band) // 2
    span = BLOCK + 2 * pad
    reach = (taps - 1) // 2
    inner = DEPTH // span
    outer = -(-taps // inner)
    tiles = side // TILE
    width = side + TILE
    blocks = band // BLOCK
    row = row_ref[0]
    core = row & 1

    if first:
        for numer in numers.values():
            numer[...] = jnp.zeros_like(numer)
    if warp:
        for g in range(count):
            image, extended = refs[g], refs[count + g]
            index = start + g
            there = core * pixels_ref.shape[0] + index
            shards = (pixels_ref.at[index], passed_ref.at[there])
            for mask, shard in enumerate(shards + (far_ref.at[g], cross_ref.at[g])):
                at = pl.multiple_of((row ^ mask) * band, band)
                image[pl.ds(at, band), :] = shard[...]
            edge = edge_ref[index]
            blank = jnp.zeros_like(edge)
            extended[0:pad, :] = jnp.where(row >= 2, edge, blank)
            extended[pad + 2 * band :, :] = jnp.where(row >= 2, blank, edge)
            for which, rows in enumerate((rows_ref.at[index], passed_rows_ref.at[there])):
                at = pl.multiple_of(pad + (core ^ which) * band, ALIGN)
                extended[pl.ds(at, band), :] = rows[...]
    for g in range(count):
        profiles = None
        for b in range(inner):
            part = profile_ref[start + g, pl.ds(b, outer, stride=inner), :]
            part = jnp.concatenate([part, jnp.zeros((outer, DEPTH - TILE), F32)], axis=1)
            part = pltpu.roll(part, span * b, 1) if b else part
            profiles = part if profiles is None else profiles + part
        for a in range(outer):
            profile = jnp.broadcast_to(profiles[a : a + 1, :], (BLOCK, DEPTH))
            toeplitz = pltpu.roll(profile, 0, 1, stride=1, stride_axis=0)
            tables[g][BLOCK * a : BLOCK * (a + 1), :] = toeplitz.astype(BF16)
    for g in range(count):
        if warp:
            image, extended = refs[g], refs[count + g]
            by_rows = jnp.dot(extended[...], image[...], preferred_element_type=F32).astype(BF16)
            warped = jnp.dot(by_rows, cols_ref[start + g], preferred_element_type=F32)
            warped_ref[g] = warped.astype(BF16)
        for m in halves:
            at = pl.multiple_of((core ^ m) * band, band)
            ring = warped_ref[g, pl.ds(at, band + 2 * pad), :]
            ring = jnp.concatenate([ring, jnp.zeros((band + 2 * pad, TILE), BF16)], axis=1)
            stack = stacks[m][g]
            if span * inner < DEPTH:
                rest = (blocks, DEPTH - span * inner, width)
                stack[:, span * inner :, :] = jnp.zeros(rest, BF16)
            for b in range(inner):
                turn = (inner // 2 - b) % width
                shifted = pltpu.roll(ring, turn, 1) if turn else ring
                for k in range(blocks):
                    stack[k, span * b : span * (b + 1), :] = shifted[BLOCK * k : BLOCK * k + span]
    middle = outer // 2
    origin = inner * middle + inner // 2 - reach
    for m in halves:
        for g in range(count):
            index = start + g
            weight = weight_ref[index]
            for k in range(blocks):
                partial = jnp.dot(tables[g][...], stacks[m][g][k], preferred_element_type=F32)
                total = None
                for a in range(outer):
                    turn = (inner * (middle - a) - origin) % width
                    part = partial[BLOCK * a : BLOCK * (a + 1)]
                    part = pltpu.roll(part, turn, 1) if turn else part
                    total = part if total is None else total + part
                matched = total[:, 0:side]
                here = slice(BLOCK * k, BLOCK * (k + 1))
                matched_refs[m][index, here, :] = matched
                for q in range(tiles):
                    slot = slot_ref[index * tiles + q]
                    piece = (weight * matched[:, TILE * q : TILE * (q + 1)]).astype(BF16)
                    numers[m][slot, here, :] += piece.astype(F32)
    if send:
        sent_ref[...] = numers[1][...].astype(BF16)


def match_chunk(scalars, profiles, operands, carry, start, count, taps, slot_count, halves, send=False):
    warp = len(operands) > 1
    if warp:
        half, band, side = operands[0].shape
        tall = 2 * band + 2 * operands[-1].shape[1]
    else:
        _, tall, side = operands[0].shape
        half, band, _ = carry[0].shape
    inner = DEPTH // (BLOCK + tall - 2 * band)
    outer = -(-taps // inner)
    width = side + TILE
    blocks = band // BLOCK
    first = carry is None
    in_vmem = pl.BlockSpec(memory_space=pltpu.VMEM)
    arrays = list(scalars) + [profiles] + list(operands)
    in_specs = [pl.BlockSpec(memory_space=pltpu.SMEM)] * 3 + [in_vmem] * (len(operands) + 1)
    aliases = {}
    if not first:
        aliases = {len(arrays) + i: i for i in range(len(carry))}
        arrays += list(carry)
        in_specs += [in_vmem] * len(carry)
    matched = jax.ShapeDtypeStruct((half, band, side), F32)
    numer_shape = (slot_count, band, TILE)
    out_shape = [matched] * len(halves) + [jax.ShapeDtypeStruct(numer_shape, F32)] * len(halves)
    if send:
        out_shape.append(jax.ShapeDtypeStruct(numer_shape, BF16))
        out_shape.append(jax.ShapeDtypeStruct((count, tall, side), BF16))
    scratch = [pltpu.VMEM((outer * BLOCK, DEPTH), BF16)] * count
    scratch += [pltpu.VMEM((blocks, DEPTH, width), BF16)] * (count * len(halves))
    if warp:
        scratch += [pltpu.VMEM((side, side), BF16)] * count
        scratch += [pltpu.VMEM((tall, side), BF16)] * count
        if not send:
            scratch.append(pltpu.VMEM((count, tall, side), BF16))
    return pl.pallas_call(
        functools.partial(
            match_kernel,
            start=start,
            count=count,
            taps=taps,
            halves=halves,
            first=first,
            warp=warp,
            send=send,
        ),
        in_specs=in_specs,
        out_specs=[in_vmem] * len(out_shape),
        scratch_shapes=scratch,
        out_shape=out_shape,
        input_output_aliases=aliases,
        compiler_params=pltpu.CompilerParams(vmem_limit_bytes=VMEM),
        cost_estimate=pl.CostEstimate(
            flops=count * 1000000000 * len(halves), bytes_accessed=count * 1000000, transcendentals=0
        ),
    )(*arrays)


def merge_kernel(own_ref, other_ref, *part_refs):
    each = part_refs[0].shape[0]
    for m, part in enumerate(part_refs):
        boxes = slice(each * m, each * (m + 1))
        part[...] = (own_ref[boxes] + other_ref[boxes].astype(F32)).astype(part.dtype)


def add_kernel(own_ref, other_ref, total_ref):
    total_ref[...] = (own_ref[...] + other_ref[...].astype(F32)).astype(BF16)


def template_kernel(denom_ref, _, *refs):
    part_refs, template_ref = refs[:-2], refs[-2]
    for q in range(template_ref.shape[0]):
        total = part_refs[0][q].astype(F32)
        for part in part_refs[1:]:
            total = total + part[q].astype(F32)
        box = (total / jnp.maximum(denom_ref[q], 1.0)).astype(BF16)
        template_ref[q] = box


def coadd_kernel(template_ref, coadd_ref):
    for q in range(template_ref.shape[0]):
        coadd_ref[:, TILE * q : TILE * (q + 1)] = template_ref[q]


def difference_kernel(slot_ref, row_ref, own_ref, other_ref, *refs, group, masks):
    template_refs, out_ref = refs[:-4], refs[-4]
    held, ready, sems = refs[-3:]
    each = template_refs[0].shape[0]
    half, _, side = own_ref.shape
    tiles = side // TILE
    core = row_ref[0] & 1
    for m, template in zip(masks, template_refs):
        held[each * m : each * (m + 1)] = template[...]
    copies = []
    for which, matched_ref in enumerate((own_ref, other_ref)):
        for first in range(0, half, group):
            at = (core ^ which) * half + first
            for i in range(group):
                for q in range(tiles):
                    slot = slot_ref[(at + i) * tiles + q]
                    columns = slice(TILE * q, TILE * (q + 1))
                    box = held[slot].astype(F32)
                    value = (matched_ref[first + i, :, columns] - box).astype(BF16)
                    ready[which * half + first + i, :, columns] = value
            copies.append(
                pltpu.make_async_copy(
                    ready.at[pl.ds(which * half + first, group)],
                    out_ref.at[pl.ds(at, group)],
                    sems.at[len(copies)],
                )
            )
            copies[-1].start()
    for copy in copies:
        copy.wait()


def exchange(value, axis, mask):
    size = lax.axis_size(axis)
    return lax.ppermute(value, axis, [(i, i ^ mask) for i in range(size)])


def per_device(
    images,
    warp_rows,
    warp_cols,
    psf_coef,
    taps,
    dest_patch,
    dest_block,
    weight_index,
    weight_table,
    patch_home,
):
    det_count, visit_count, band, side = images.shape
    kernel_count, tap_count = taps.shape
    reach = (tap_count - 1) // 2
    pad = -(-reach // ALIGN) * ALIGN
    span = BLOCK + 2 * pad
    tiles = side // TILE
    det_devices = lax.axis_size("det")
    mine = lax.axis_index("det")
    row = lax.axis_index("row").astype(jnp.int32)
    core = row & 1
    image_count = det_count * visit_count
    half = image_count // 2
    assert lax.axis_size("row") == 4 and image_count == 2 * half
    pixels = images.reshape(image_count, band, side)
    rows = warp_rows.reshape(image_count, band, side)
    cols = warp_cols.reshape(image_count, side, side)
    row_one = row.reshape(1)

    chunks = CHUNKS if sum(CHUNKS) == half else (1,) * half
    starts = [sum(chunks[:c]) for c in range(len(chunks))]
    spans = list(zip(starts, chunks))
    far, cross = [], []

    def send(packed):
        for first, second in zip(packed[::2], packed[1::2]):
            far.append(exchange(first, "row", 2))
            cross.append(exchange(second, "row", 3))

    send(pack(row_one, pixels, rows, spans[:1], pad))
    sibling_rows = exchange(rows, "row", 1)
    sibling_pixels = exchange(pixels, "row", 1)
    packed = pack(row_one, pixels, rows, spans[-1:], pad, sibling_rows=sibling_rows)
    edge = exchange(packed[-1], "row", 2)
    send(pack(row_one, pixels, rows, spans[1:-1], pad, after=[far[0]]))
    send(packed[:-1])

    with jax.named_scope("profiles"):
        scaled = (psf_coef.reshape(image_count, kernel_count)[:, :, None] * taps).astype(BF16)
        profiles = jnp.einsum(
            "nkt,ku->nut", scaled, taps.astype(BF16), preferred_element_type=F32
        )
        inner = DEPTH // span
        rows_kept = -(-tap_count // inner) * inner
        profiles = jnp.pad(
            profiles,
            (
                (0, 0),
                (0, rows_kept - tap_count + -rows_kept % 8),
                (pad - reach, TILE - tap_count - pad + reach),
            ),
        )
    anywhere = pl.BlockSpec(memory_space=pl.ANY)
    in_vmem = pl.BlockSpec(memory_space=pltpu.VMEM)
    large = (pixels, rows, cols, profiles)
    slots, own_slots, weights, denom, *kept = pl.pallas_call(
        functools.partial(target_kernel, tiles=tiles),
        in_specs=[pl.BlockSpec(memory_space=pltpu.SMEM)] * 6 + [anywhere] * 5,
        out_specs=[pl.BlockSpec(memory_space=pltpu.SMEM)] * 4 + [in_vmem] * 4,
        out_shape=[
            jax.ShapeDtypeStruct((image_count * tiles,), jnp.int32),
            jax.ShapeDtypeStruct((half * tiles,), jnp.int32),
            jax.ShapeDtypeStruct((half,), F32),
            jax.ShapeDtypeStruct((tiles,), F32),
        ]
        + [jax.ShapeDtypeStruct((half,) + a.shape[1:], a.dtype) for a in large],
        scratch_shapes=[pltpu.SemaphoreType.DMA((len(large),))],
        compiler_params=pltpu.CompilerParams(vmem_limit_bytes=VMEM),
    )(
        jnp.stack([mine.astype(jnp.int32), row]),
        dest_patch.reshape(-1),
        dest_block,
        weight_index.T,
        weight_table,
        patch_home,
        *[pltpu.with_memory_space_constraint(a, pltpu.HBM) for a in large],
        packed[-1],
    )

    carry = None
    slot_count = det_devices * tiles
    scalars = (own_slots, weights, row_one)
    common = (tap_count, slot_count)
    for c, (s, n) in enumerate(spans):
        operands = tuple(kept[:3]) + (sibling_pixels, sibling_rows, far[c], cross[c], edge)
        if c < len(spans) - 1:
            carry = match_chunk(scalars, kept[3], operands, carry, s, n, *common, (0, 1))
    matched_sent, _, sums_sent, warped = match_chunk(
        scalars, kept[3], operands, carry[1::2], s, n, *common, (1,), send=True
    )
    other_sums = exchange(sums_sent, "row", 1)
    matched, own_sums = match_chunk(
        scalars, kept[3], (warped,), carry[0::2], s, n, *common, (0,)
    )
    box_shape = (tiles, band, TILE)
    box = jax.ShapeDtypeStruct(box_shape, BF16)
    small = pltpu.CompilerParams(vmem_limit_bytes=4 * MIB + 16 * slot_count * band * TILE)
    parts = pl.pallas_call(
        merge_kernel,
        in_specs=[in_vmem] * 2,
        out_specs=[in_vmem] * det_devices,
        out_shape=[
            jax.ShapeDtypeStruct(box_shape, BF16 if m % 2 else F32) for m in range(det_devices)
        ],
        compiler_params=small,
    )(own_sums, other_sums)
    evens = tuple(range(2, det_devices, 2))
    across = {m: exchange(parts[m ^ 1], "det", 1) for m in evens + (0,)}
    received = [parts[0], across[0]]
    for m in evens:
        total = pl.pallas_call(
            add_kernel,
            in_specs=[in_vmem] * 2,
            out_specs=in_vmem,
            out_shape=box,
            compiler_params=small,
        )(parts[m], across[m])
        received.append(exchange(total, "det", m))
    template, matched_sent = pl.pallas_call(
        template_kernel,
        in_specs=[pl.BlockSpec(memory_space=pltpu.SMEM), anywhere] + [in_vmem] * len(received),
        out_specs=[in_vmem, anywhere],
        out_shape=[
            box,
            jax.ShapeDtypeStruct(matched_sent.shape, F32),
        ],
        input_output_aliases={1: 1},
        compiler_params=small,
    )(denom, matched_sent, *received)
    other_matched = exchange(matched_sent, "row", 1)
    passed = {0: template}
    for m in evens:
        passed[m] = exchange(template, "det", m)
    for m in evens + (0,):
        passed[m ^ 1] = exchange(passed[m], "det", 1)
    masks = tuple(range(det_devices - 1, -1, -1))
    templates = [passed[m] for m in masks]
    coadd = pl.pallas_call(
        coadd_kernel,
        in_specs=[in_vmem],
        out_specs=in_vmem,
        out_shape=jax.ShapeDtypeStruct((band, side), BF16),
        compiler_params=small,
    )(template)
    group = 3 if half % 3 == 0 else 1
    difference = pl.pallas_call(
        functools.partial(difference_kernel, group=group, masks=masks),
        in_specs=[pl.BlockSpec(memory_space=pltpu.SMEM)] * 2 + [in_vmem] * (2 + det_devices),
        out_specs=anywhere,
        scratch_shapes=[
            pltpu.VMEM((slot_count, band, TILE), BF16),
            pltpu.VMEM((image_count, band, side), BF16),
            pltpu.SemaphoreType.DMA((image_count // group,)),
        ],
        out_shape=jax.ShapeDtypeStruct((image_count, band, side), BF16),
        compiler_params=small,
    )(slots, row_one, matched, other_matched, *templates)
    return difference.reshape(images.shape), coadd.reshape(1, band, side)


def solution(mesh):
    placed = (
        P("det", None, "row", None),
        P("det", None, "row", None),
        P("det", None, None, None),
        P("det", None, None),
        P(),
        P(),
        P(),
        P(),
        P(),
        P(),
    )
    return jax.shard_map(
        per_device,
        mesh=mesh,
        in_specs=placed,
        out_specs=(P("det", None, "row", None), P("det", "row", None)),
        check_vma=False,
    )
```
